32 devices in a mesh: member: 4 (over z), region: 8 (over y, x, core).
Axes of the slice: x: 2, y: 2, z: 4, core: 2. Of those that a mesh axis runs over, the one named last changes fastest.
Arguments:
- grid_input: bfloat16 [16, 4096, 1024], P('member', 'region'), may hold values from -6 to 6
- w_hidden: bfloat16 [1024, 1024], replicated, may hold values from -0.1875 to 0.1875
- b_hidden: float32 [1024], replicated, may hold values from -3 to 3
- w_out: bfloat16 [1024, 96], replicated, may hold values from -0.1875 to 0.1875
- b_out: float32 [96], replicated, may hold values from -3 to 3
- target: float32 [96, 4096], P(None, 'region'), may hold values from -6 to 6
- channel_weight: float32 [96], replicated, may hold values from 0.5 to 5
- interp_weight: bfloat16 [32, 3, 128, 128], P('region'), may hold values from -0.5 to 0.5
- block_index: int32 [32, 3], P('region'), may hold values from 0 to 15, as said below
Outputs:
- grad_w_hidden: float32 [1024, 1024], P(('member', 'region'))
- grad_w_out: float32 [1024, 96], P(('member', 'region'))
- grad_mesh: float32 [16, 2048, 1024], P('member', 'region')
The draws below stay inside these ranges and needn't reach their ends.
Inputs may be any that keep to these rules, and one draw needn't show every extreme that they name: `block_index`: grid block b lies in region b // 4; its mesh blocks belong to that region or to one of its two neighbours along the region index, cyclically, a block j belonging to region j // 2. For k = 0 the mesh block is the region's own block number (b % 4) % 2.
All inputs are finite; a program needn't handle non-finite values.
Results may differ from the reference program's by a relative error of at most 0.0095.
Values may be sent and summed in bfloat16 or wider, within the bound.
No kernel may reach another device: no remote copies, remote signals or barrier semaphores. Data moves between devices by JAX's collectives and lax.ppermute only.
A program may use at most 128 MiB of HBM per device.

```python
import math
import jax
import jax.numpy as jnp
from jax import lax

M = 16
H = 1024
C = 96
GB = 128
MB = 128
K = 3
GBLK_REG = 4
MBLK_REG = 2
NGB = 32
NMB = 16
NCELL = 4096
NMESH = 2048


def draw_block_index(key, part):
    position = jnp.arange(NGB, dtype=jnp.int32)
    region_of = position // GBLK_REG
    local_pos = position % GBLK_REG
    regions = NMB // MBLK_REG
    key_offset, key_within = jax.random.split(key)
    offset = jax.random.randint(key_offset, (NGB, K), -1, 2).astype(jnp.int32)
    within = jax.random.randint(key_within, (NGB, K), 0, MBLK_REG).astype(jnp.int32)
    first = (jnp.arange(K, dtype=jnp.int32) == 0)[None, :]
    offset = jnp.where(first, 0, offset)
    within = jnp.where(first, (local_pos % MBLK_REG)[:, None], within)
    owner = (region_of[:, None] + offset + regions) % regions
    return (owner * MBLK_REG + within).astype(jnp.int32)


def steps_of(own_key, extent, pieces, low, high):
    level = 1.0
    for dim, parts in pieces:
        draws = jax.random.uniform(jax.random.fold_in(jax.random.fold_in(own_key, 6), dim), (parts,), jnp.float32, low / len(pieces), high / len(pieces))
        level = level * jnp.repeat(jnp.exp(draws), extent[dim] // parts).reshape((-1,) + (1,) * (len(extent) - 1 - dim))
    return level


def centred(key, shape, scale, reach, pieces=(), kind=jnp.bfloat16):
    gain = steps_of(key, shape, pieces, -0.22, 0.18) if pieces else 1.0
    entries = jax.random.normal(key, shape, jnp.float32) * scale * gain
    return jnp.minimum(jnp.maximum(entries, -reach), reach).astype(kind)


def setup_inputs(seed: int = 0) -> dict:
    seeds = jax.random.split(jax.random.key(seed), 10)
    return {
        "grid_input": centred(seeds[0], (M, NCELL, H), 1.0, 6.0, ((0, 4), (1, 8))),
        "w_hidden": centred(seeds[1], (H, H), H ** -0.5, 0.1875),
        "b_hidden": centred(seeds[2], (H,), 0.5, 3.0, (), jnp.float32),
        "w_out": centred(seeds[3], (H, C), H ** -0.5, 0.1875),
        "b_out": centred(seeds[4], (C,), 0.5, 3.0, (), jnp.float32),
        "target": centred(seeds[5], (C, NCELL), 1.0, 6.0, ((1, 8),), jnp.float32),
        "channel_weight": jnp.clip(jnp.exp(jax.random.uniform(seeds[6], (C,), jnp.float32, math.log(0.5), math.log(5.0))), 0.5, 5.0),
        "interp_weight": centred(seeds[7], (NGB, K, GB, MB), MB ** -0.5, 0.5, ((0, 8),)),
        "block_index": draw_block_index(jax.random.fold_in(seeds[9], 71), 0),
    }


ALPHA = 0.95
SMOOTH = 0.25

def smooth_slope(diff):
    return diff / jnp.sqrt(diff * diff + SMOOTH * SMOOTH)

def ensemble_adjoint(own, every, target_cells, channel_weight):
    members = every.shape[0]
    kappa = ALPHA / (2.0 * members * (members - 1)) + (1.0 - ALPHA) / (2.0 * members * members)
    skill = smooth_slope(own - target_cells[None]) / members
    spread = lax.optimization_barrier(jnp.sum(smooth_slope(own[:, None] - every[None, :]), axis=1))
    return channel_weight[None, :, None] * (skill - 2.0 * kappa * spread)

def reference(grid_input, w_hidden, b_hidden, w_out, b_out, target, channel_weight, interp_weight, block_index):

    def forward(member_input):
        pre_act = jnp.dot(member_input, w_hidden, preferred_element_type=jnp.float32) + b_hidden
        activated = jax.nn.silu(pre_act).astype(jnp.bfloat16)
        return jnp.dot(activated, w_out, preferred_element_type=jnp.float32) + b_out
    predicted = lax.map(forward, grid_input)
    pred_blocks = predicted.reshape(M, NGB, GB, C).transpose(1, 0, 3, 2)
    target_blocks = target.reshape(C, NGB, GB).transpose(1, 0, 2)

    def score_block(pair):
        return ensemble_adjoint(pair[0], pair[0], pair[1], channel_weight)
    adjoint = lax.map(score_block, (pred_blocks, target_blocks))
    dpred_all = adjoint.astype(jnp.bfloat16).transpose(1, 0, 3, 2).reshape(M, NCELL, C)
    tiles = interp_weight.astype(jnp.float32)
    flat_index = block_index.reshape(-1).astype(jnp.int32)

    def backward(pair):
        member_input, member_dpred = pair
        pre_act = jnp.dot(member_input, w_hidden, preferred_element_type=jnp.float32) + b_hidden
        activated = jax.nn.silu(pre_act).astype(jnp.bfloat16)
        dact = jnp.dot(member_dpred, w_out.T, preferred_element_type=jnp.float32)
        logistic = jax.nn.sigmoid(pre_act)
        dpre = (dact * logistic * (1.0 + pre_act * (1.0 - logistic))).astype(jnp.bfloat16)
        dinput = jnp.dot(dpre, w_hidden.T, preferred_element_type=jnp.float32).astype(jnp.bfloat16)
        grad_hidden = jnp.dot(member_input.T, dpre, preferred_element_type=jnp.float32)
        grad_output = jnp.dot(activated.T, member_dpred, preferred_element_type=jnp.float32)
        blocks = dinput.reshape(NGB, GB, H).astype(jnp.float32)
        contrib = jnp.einsum('bkgn,bgh->bknh', tiles, blocks, precision=lax.Precision.HIGHEST)
        mesh = jax.ops.segment_sum(contrib.reshape(NGB * K, MB, H), flat_index, num_segments=NMB)
        return (grad_hidden, grad_output, mesh.reshape(NMESH, H))
    grads_hidden, grads_output, grad_mesh = lax.map(backward, (grid_input, dpred_all))
    return (lax.optimization_barrier(jnp.sum(grads_hidden, axis=0)), lax.optimization_barrier(jnp.sum(grads_output, axis=0)), grad_mesh)
```

```python
import functools

import jax
import jax.numpy as jnp
from jax import lax
from jax.experimental import pallas as pl
from jax.experimental.pallas import tpu as pltpu
from jax.sharding import PartitionSpec as P

ALPHA = 0.95
SMOOTH = 0.25
MBLK_REG = 2
PER = 1
SCOPED = 16 * 1024 * 1024
F32 = jnp.float32
BF16 = jnp.bfloat16
ON_VMEM = pl.BlockSpec(memory_space=pltpu.VMEM)
ON_HBM = pl.BlockSpec(memory_space=pltpu.HBM)
ON_SMEM = pl.BlockSpec(memory_space=pltpu.SMEM)
ANYWHERE = pl.BlockSpec(memory_space=pl.ANY)


def shifted(block, axis, distance):
    count = lax.axis_size(axis)
    return lax.ppermute(block, axis, [((i - distance) % count, i) for i in range(count)])


def exchanged(block, axis, bit):
    count = lax.axis_size(axis)
    return lax.ppermute(block, axis, [(i, i ^ bit) for i in range(count)])


def smooth_slope(diff):
    return diff * lax.rsqrt(diff * diff + SMOOTH * SMOOTH)


def params():
    return pltpu.CompilerParams(vmem_limit_bytes=SCOPED)


def cost(flops, moved):
    return pl.CostEstimate(flops=int(flops), bytes_accessed=int(moved), transcendentals=0)


def forward_kernel(
    pieces, place, x_hbm, w_hbm, b_ref, wout_ref, x_ref, w_ref, act_ref, slope_ref, *rest
):
    sends, line, base, x_sems, w_sems = rest[:pieces], *rest[pieces:]
    members, _, width = x_ref.shape
    length = sends[0].shape[2]
    step = width // w_sems.shape[0]
    w_parts = [slice(lo, lo + step) for lo in range(0, width, step)]
    w_copies = [
        pltpu.make_async_copy(w_hbm.at[:, cols], w_ref.at[:, cols], w_sems.at[i])
        for i, cols in enumerate(w_parts)
    ]
    x_copies = [pltpu.make_async_copy(x_hbm.at[m], x_ref.at[m], x_sems.at[m]) for m in range(members)]
    x_copies[0].start()
    for copy in w_copies + x_copies[1:]:
        copy.start()
    for m in range(members):
        x_copies[m].wait()
        row = None
        for i, cols in enumerate(w_parts):
            if m == 0:
                w_copies[i].wait()
            pre = jnp.dot(x_ref[m], w_ref[:, cols], preferred_element_type=F32) + b_ref[:, cols]
            logistic = 0.5 * jnp.tanh(0.5 * pre) + 0.5
            act = pre * logistic
            slope_ref[m, :, cols] = (logistic + act * (1.0 - logistic)).astype(BF16)
            act = act.astype(BF16)
            act_ref[m, :, cols] = act
            part = lax.dot_general(
                wout_ref[:, cols], act, (((1,), (1,)), ((), ())), preferred_element_type=F32
            )
            row = part if row is None else row + part
        if m == 0:
            base[...] = row.astype(BF16).astype(F32)
        line[m] = row - base[...]
    for s in range(pieces):
        at = lax.rem(place[0] + s, pieces) * length
        lanes = pl.ds(pl.multiple_of(at, length), length)
        sends[s][0] = base[:, lanes].astype(BF16)
        for m in range(members):
            sends[s][1 + m] = line[m, :, lanes].astype(BF16)


def forward(grid_input, w_hidden, b_hidden, w_out_t, place, pieces):
    members, cells, width = grid_input.shape
    channels = w_out_t.shape[0]
    length = cells // pieces
    return pl.pallas_call(
        functools.partial(forward_kernel, pieces),
        in_specs=[ON_SMEM, ON_HBM, ON_HBM, ON_VMEM, ON_VMEM],
        out_specs=[ON_VMEM] * (4 + pieces),
        out_shape=[
            pltpu.VMEM(grid_input.shape, BF16),
            pltpu.VMEM(w_hidden.shape, BF16),
            pltpu.VMEM(grid_input.shape, BF16),
            pltpu.VMEM(grid_input.shape, BF16),
        ]
        + [pltpu.VMEM((members + 1, channels, length), BF16)] * pieces,
        scratch_shapes=[
            pltpu.VMEM((members, channels, cells), F32),
            pltpu.VMEM((channels, cells), F32),
            pltpu.SemaphoreType.DMA((members,)),
            pltpu.SemaphoreType.DMA((2,)),
        ],
        compiler_params=params(),
        cost_estimate=cost(2 * members * cells * width * (width + 256), 14 << 20),
        name="forward",
    )(place, grid_input, w_hidden, b_hidden.reshape(1, width), w_out_t)


def score_kernel(pieces, place, target_ref, bias_ref, weight_ref, *refs):
    given, out, (bias, weights_of) = refs[:pieces], refs[pieces : 2 * pieces], refs[2 * pieces :]
    per, channels, length = out[0].shape
    members = per * pieces
    kappa = ALPHA / (2.0 * members * (members - 1)) + (1.0 - ALPHA) / (2.0 * members * members)
    start = pl.multiple_of(place[0] * length, length)
    bias[...] = jnp.broadcast_to(bias_ref[...], (8, channels)).T
    weights_of[...] = jnp.broadcast_to(weight_ref[...], (8, channels)).T

    def rows_step(i, carry):
        rows = pl.ds(pl.multiple_of(i * 16, 16), 16)
        own = []
        for s in range(pieces):
            base = given[s][0, rows, :].astype(F32)
            own += [base + given[s][1 + m, rows, :].astype(F32) for m in range(per)]
        aim = target_ref[rows, pl.ds(start, length)] - bias[rows, :1]
        weight = weights_of[rows, :1]
        spread = [None] * members
        for j in range(members):
            for k in range(j + 1, members):
                slope = smooth_slope(own[j] - own[k])
                spread[j] = slope if spread[j] is None else spread[j] + slope
                spread[k] = -slope if spread[k] is None else spread[k] - slope
        for j in range(members):
            skill = smooth_slope(own[j] - aim) * (1.0 / members)
            value = weight * (skill - (2.0 * kappa) * spread[j])
            out[j // per][j % per, rows, :] = value.astype(BF16)
        return carry

    lax.fori_loop(0, channels // 16, rows_step, 0)


def score(given, target, b_out, channel_weight, place):
    pieces = len(given)
    extra, channels, length = given[0].shape
    shape = (extra - 1, channels, length)
    return pl.pallas_call(
        functools.partial(score_kernel, pieces),
        in_specs=[ON_SMEM] + [ON_VMEM] * (3 + pieces),
        out_specs=[ON_VMEM] * pieces,
        out_shape=[pltpu.VMEM(shape, BF16)] * pieces,
        scratch_shapes=[pltpu.VMEM((channels, 8), F32)] * 2,
        compiler_params=params(),
        cost_estimate=cost(40_000_000, 1 << 20),
        name="score",
    )(place, target, b_out.reshape(1, channels), channel_weight.reshape(1, channels), *given)


def tiles_kernel(per_region, regions, place, index_ref, tile_ref, out_ref, total):
    blocks, sources, cells, nodes = tile_ref.shape
    total[...] = jnp.zeros_like(total)
    for b in range(blocks):
        for k in range(sources):
            number = index_ref[b, k]
            relative = lax.rem(number // per_region - place[1] + 1 + regions, regions)
            slot = relative * per_region + lax.rem(number, per_region)
            total[slot, b] += tile_ref[b, k].astype(F32).T
    for s in range(total.shape[0]):
        for b in range(blocks):
            out_ref[s * nodes : (s + 1) * nodes, b * cells : (b + 1) * cells] = total[s, b].astype(BF16)


def tiles_matrix(interp_weight, block_index, place, per_region, regions):
    blocks, _, cells, nodes = interp_weight.shape
    slots = 3 * per_region
    return pl.pallas_call(
        functools.partial(tiles_kernel, per_region, regions),
        in_specs=[ON_SMEM, ON_SMEM, ON_VMEM],
        out_specs=ON_VMEM,
        out_shape=pltpu.VMEM((slots * nodes, blocks * cells), BF16),
        scratch_shapes=[pltpu.VMEM((slots, blocks, nodes, cells), F32)],
        compiler_params=params(),
        cost_estimate=cost(4_000_000, 2 << 20),
        name="tiles",
    )(place, block_index, interp_weight)


def backward_kernel(first, pieces, place, wout_ref, slope_ref, tiles_ref, *refs):
    given = refs[:pieces]
    dpred_ref, dpre_ref, below_ref, own_ref, above_ref = refs[pieces:]
    length = given[0].shape[2]
    members, nodes, width = own_ref.shape
    step = 512
    for m in range(members):
        for s in range(pieces):
            at = lax.rem(place[0] + s, pieces) * length
            rows = pl.ds(pl.multiple_of(at, length), length)
            dpred_ref[m, rows, :] = given[s][first + m].astype(F32).T.astype(BF16)
        for lo in range(0, width, step):
            cols = slice(lo, lo + step)
            dact = jnp.dot(dpred_ref[m], wout_ref[:, cols], preferred_element_type=F32)
            dpre = (dact * slope_ref[first + m, :, cols].astype(F32)).astype(BF16)
            dpre_ref[m, :, cols] = dpre
            terms = jnp.dot(tiles_ref[...], dpre, preferred_element_type=F32)
            below_ref[m, :, cols] = terms[:nodes].astype(BF16)
            own_ref[m, :, cols] = terms[nodes : 2 * nodes].astype(BF16)
            above_ref[m, :, cols] = terms[2 * nodes :].astype(BF16)


def backward(first, members, given, w_out_t, slope, tiles, place):
    pieces = len(given)
    _, cells, width = slope.shape
    channels = w_out_t.shape[0]
    nodes = tiles.shape[0] // 3
    return pl.pallas_call(
        functools.partial(backward_kernel, first, pieces),
        in_specs=[ON_SMEM] + [ON_VMEM] * (3 + pieces),
        out_specs=[ON_VMEM] * 5,
        out_shape=[
            pltpu.VMEM((members, cells, channels), BF16),
            pltpu.VMEM((members, cells, width), BF16),
            pltpu.VMEM((members, nodes, width), BF16),
            pltpu.VMEM((members, nodes, width), BF16),
            pltpu.VMEM((members, nodes, width), BF16),
        ],
        compiler_params=params(),
        cost_estimate=cost(2 * members * cells * width * (256 + 3 * nodes), 5 << 20),
        name="backward",
    )(place, w_out_t, slope, tiles, *given)


def weights_kernel(parts, cores, place, x_ref, act_ref, *refs):
    dpre, dpred = refs[:parts], refs[parts : 2 * parts]
    per, _, width = dpre[0].shape
    across = (((0,), (0,)), ((), ()))
    step = 256
    total = refs[-1]
    count, rows = total.shape[1:3]
    for lo in range(0, width, step):
        cols = slice(lo, lo + step)
        hidden = output = None
        for m in range(parts * per):
            part = lax.dot_general(
                x_ref[m, :, cols], dpre[m // per][m % per], across, preferred_element_type=F32
            )
            hidden = part if hidden is None else hidden + part
            part = lax.dot_general(
                act_ref[m, :, cols], dpred[m // per][m % per], across, preferred_element_type=F32
            )
            output = part if output is None else output + part
        hidden, output = hidden.astype(BF16), output.astype(BF16)
        for i in range(step // rows):
            block = lo // rows + i
            total[block % cores, block // cores, :, :width] = hidden[i * rows : (i + 1) * rows]
            total[block % cores, block // cores, :, width:] = output[i * rows : (i + 1) * rows]
    if cores == 1:
        refs[2 * parts][...] = total[0]
    else:
        mine = lax.rem(place[1], cores)
        refs[2 * parts][...] = total[1 - mine]
        refs[2 * parts + 1][...] = total[mine]


def weights(x, act, dpre, dpred, place, blocks, cores):
    members, cells, width = x.shape
    columns = width + dpred[0].shape[2]
    parts = len(dpre)
    rows = width // blocks
    return pl.pallas_call(
        functools.partial(weights_kernel, parts, cores),
        in_specs=[ON_SMEM] + [ON_VMEM] * (2 + 2 * parts),
        out_specs=[ON_VMEM] * cores,
        out_shape=[pltpu.VMEM((blocks // cores, rows, columns), BF16)] * cores,
        scratch_shapes=[pltpu.VMEM((cores, blocks // cores, rows, columns), BF16)],
        compiler_params=params(),
        cost_estimate=cost(1000, 1000),
        name="weights",
    )(place, x, act, *dpre, *dpred)


def halve_kernel(which, bit, after, place, kept_ref, came_ref, away_ref, mine_ref):
    count = away_ref.shape[0]
    mine = lax.rem(place[which] // bit, 2)
    for ref, side in ((away_ref, 1 - mine), (mine_ref, mine)):
        for i in range(count):
            at = (2 * (i // after) + side) * after + i % after
            ref[i] = (kept_ref[at].astype(F32) + came_ref[at].astype(F32)).astype(BF16)


def halve(kept, came, place, which, bit, after):
    blocks, rows, columns = kept.shape
    half = pltpu.VMEM((blocks // 2, rows, columns), BF16)
    return pl.pallas_call(
        functools.partial(halve_kernel, which, bit, after),
        in_specs=[ON_SMEM, ON_VMEM, ON_VMEM],
        out_specs=[ON_VMEM] * 2,
        out_shape=[half, half],
        compiler_params=params(),
        cost_estimate=cost(1000, 1000),
        name="halve",
    )(place, kept, came)


def total_kernel(kept_ref, came_ref, hidden_ref, output_ref):
    total = kept_ref[0].astype(F32) + came_ref[0].astype(F32)
    width = hidden_ref.shape[1]
    hidden_ref[...] = total[:, :width]
    output_ref[...] = total[:, width:]


def last_total(kept, came, width):
    _, rows, columns = kept.shape
    return pl.pallas_call(
        total_kernel,
        in_specs=[ON_VMEM] * 2,
        out_specs=[ON_VMEM] * 2,
        out_shape=[
            jax.ShapeDtypeStruct((rows, width), F32),
            jax.ShapeDtypeStruct((rows, columns - width), F32),
        ],
        compiler_params=params(),
        cost_estimate=cost(1000, 1000),
        name="total",
    )(kept, came)


def bits_of(count):
    return [1 << i for i in range(count.bit_length() - 1)]


def weight_gradients(x, act, dpre, dpred, place, after):
    groups, regions = lax.axis_size("member"), lax.axis_size("region")
    blocks, width = groups * regions, x.shape[2]
    if regions < 2 or blocks & (blocks - 1) or (width // blocks) % 16:
        (part,) = weights(x, act, dpre, dpred, place, blocks, 1)
        part = part.reshape(width, -1)
        part = lax.psum_scatter(part, "member", scatter_dimension=0, tiled=True)
        part = lax.psum_scatter(part, "region", scatter_dimension=0, tiled=True).astype(F32)
        return part[:, :width], part[:, width:]
    near, *far = [(1, b) for b in bits_of(regions)]
    line = [(0, b) for b in bits_of(groups)]
    order = far[::-1][:1] + line + far[::-1][1:]
    names = line[::-1] + far[::-1]
    axes = ("member", "region")
    away, kept = weights(x, act, dpre, dpred, place, blocks, 2)
    (away, kept), _ = lax.optimization_barrier(((away, kept), after))
    came = exchanged(away, "region", 1)
    for which, bit in order:
        at = names.index((which, bit))
        names.pop(at)
        away, kept = halve(kept, came, place, which, bit, 1 << (len(names) - at))
        came = exchanged(away, axes[which], bit)
    return last_total(kept, came, width)


def finish_kernel(own_ref, up_ref, down_ref, w_ref, *refs):
    out_ref = refs[-1]
    total = own_ref[0].astype(F32) + up_ref[0].astype(F32) + down_ref[0].astype(F32)
    out_ref[0] = lax.dot_general(
        total.astype(BF16), w_ref[...], (((1,), (1,)), ((), ())), preferred_element_type=F32
    )


def finish(first, members, own, up, down, w_hidden, held):
    here, nodes, width = own.shape
    step = 128
    rows = pl.BlockSpec((1, step, width), lambda m, j: (m, j, 0))
    extra = [] if held is None else [held]
    return pl.pallas_call(
        finish_kernel,
        grid=(here, nodes // step),
        in_specs=[rows, rows, rows, pl.BlockSpec((width, width), lambda m, j: (0, 0))]
        + [ANYWHERE] * len(extra),
        out_specs=pl.BlockSpec((1, step, width), lambda m, j: (first + m, j, 0)),
        out_shape=jax.ShapeDtypeStruct((members, nodes, width), F32),
        input_output_aliases={4: 0} if extra else {},
        compiler_params=params(),
        cost_estimate=cost(1000, 1000),
        name="finish",
    )(own, up, down, w_hidden, *extra)


def body(
    grid_input, w_hidden, b_hidden, w_out, b_out, target, channel_weight, interp_weight, block_index
):
    members, cells, width = grid_input.shape
    groups, regions = lax.axis_size("member"), lax.axis_size("region")
    per_region = MBLK_REG
    place = jnp.stack([lax.axis_index("member"), lax.axis_index("region")]).astype(jnp.int32)
    w_out_t = w_out.T
    tiles = tiles_matrix(interp_weight, block_index, place, per_region, regions)
    x, w_hidden, act, slope, *sends = forward(grid_input, w_hidden, b_hidden, w_out_t, place, groups)
    given = [sends[0]] + [shifted(sends[s], "member", s) for s in range(1, groups)]
    adjoint = score(given, target, b_out, channel_weight, place)
    back = [adjoint[0]] + [shifted(adjoint[s], "member", -s) for s in range(1, groups)]
    dpred, dpre, own, up, down = [], [], [], [], []
    per = PER
    for first in range(0, members, per):
        one = backward(first, per, back, w_out_t, slope, tiles, place)
        dpred.append(one[0])
        dpre.append(one[1])
        own.append(one[3])
        down.append(shifted(one[2], "region", -1))
        up.append(shifted(one[4], "region", 1))
    hidden, output = weight_gradients(x, act, dpre, dpred, place, (up[0], down[0]))
    out = None
    for i, first in enumerate(range(0, members, per)):
        out = finish(first, members, own[i], up[i], down[i], w_hidden, out)
    return hidden, output, out


def solution(mesh):
    placed = (
        P("member", "region", None),
        P(),
        P(),
        P(),
        P(),
        P(None, "region"),
        P(),
        P("region", None, None, None),
        P("region", None),
    )
    return jax.shard_map(
        body,
        mesh=mesh,
        in_specs=placed,
        out_specs=(
            P(("member", "region"), None),
            P(("member", "region"), None),
            P("member", "region", None),
        ),
        check_vma=False,
    )
```

```python
import functools

import jax
import jax.numpy as jnp
from jax import lax
from jax.experimental import pallas as pl
from jax.experimental.pallas import tpu as pltpu
from jax.sharding import PartitionSpec as P

ALPHA = 0.95
SMOOTH = 0.25
MBLK_REG = 2
SCOPED = 16 * 1024 * 1024
F32 = jnp.float32
BF16 = jnp.bfloat16
ON_VMEM = pl.BlockSpec(memory_space=pltpu.VMEM)
ON_HBM = pl.BlockSpec(memory_space=pltpu.HBM)
ON_SMEM = pl.BlockSpec(memory_space=pltpu.SMEM)
ANYWHERE = pl.BlockSpec(memory_space=pl.ANY)


def shifted(block, axis, distance):
    count = lax.axis_size(axis)
    return lax.ppermute(block, axis, [((i - distance) % count, i) for i in range(count)])


def exchanged(block, axis, bit):
    count = lax.axis_size(axis)
    return lax.ppermute(block, axis, [(i, i ^ bit) for i in range(count)])


def smooth_slope(diff):
    return diff * lax.rsqrt(diff * diff + SMOOTH * SMOOTH)


def params():
    return pltpu.CompilerParams(vmem_limit_bytes=SCOPED)


def in_hbm(array):
    return pltpu.with_memory_space_constraint(array, pltpu.HBM)


def cost(flops, moved):
    return pl.CostEstimate(flops=int(flops), bytes_accessed=int(moved), transcendentals=0)


def forward_kernel(
    pieces, place, x_hbm, w_hbm, b_ref, wout_ref, x_ref, w_ref, act_ref, slope_ref, *rest
):
    sends, line, base, x_sems, w_sem = rest[:pieces], *rest[pieces:]
    members, cells, _ = x_ref.shape
    length = sends[0].shape[2]
    w_copy = pltpu.make_async_copy(w_hbm, w_ref, w_sem)
    x_copies = [pltpu.make_async_copy(x_hbm.at[m], x_ref.at[m], x_sems.at[m]) for m in range(members)]
    w_copy.start()
    x_copies[0].start()
    w_copy.wait()
    for copy in x_copies[1:]:
        copy.start()
    step = cells // 2
    for m in range(members):
        x_copies[m].wait()
        for lo in range(0, cells, step):
            rows = slice(lo, lo + step)
            pre = jnp.dot(x_ref[m, rows, :], w_ref[...], preferred_element_type=F32) + b_ref[...]
            logistic = 0.5 * jnp.tanh(0.5 * pre) + 0.5
            act = pre * logistic
            slope_ref[m, rows, :] = (logistic + act * (1.0 - logistic)).astype(BF16)
            act = act.astype(BF16)
            act_ref[m, rows, :] = act
            part = lax.dot_general(
                wout_ref[...], act, (((1,), (1,)), ((), ())), preferred_element_type=F32
            )
            if m == 0:
                base[:, rows] = part.astype(BF16).astype(F32)
            line[m, :, rows] = part - base[:, rows]
    for s in range(pieces):
        at = lax.rem(place[0] + s, pieces) * length
        lanes = pl.ds(pl.multiple_of(at, length), length)
        sends[s][0] = base[:, lanes].astype(BF16)
        for m in range(members):
            sends[s][1 + m] = line[m, :, lanes].astype(BF16)


def forward(grid_input, w_hidden, b_hidden, w_out_t, place, pieces):
    members, cells, width = grid_input.shape
    channels = w_out_t.shape[0]
    length = cells // pieces
    return pl.pallas_call(
        functools.partial(forward_kernel, pieces),
        in_specs=[ON_SMEM, ON_HBM, ON_HBM, ON_VMEM, ON_VMEM],
        out_specs=[ON_VMEM] * (4 + pieces),
        out_shape=[
            pltpu.VMEM(grid_input.shape, BF16),
            pltpu.VMEM(w_hidden.shape, BF16),
            pltpu.VMEM(grid_input.shape, BF16),
            pltpu.VMEM(grid_input.shape, BF16),
        ]
        + [pltpu.VMEM((members + 1, channels, length), BF16)] * pieces,
        scratch_shapes=[
            pltpu.VMEM((members, channels, cells), F32),
            pltpu.VMEM((channels, cells), F32),
            pltpu.SemaphoreType.DMA((members,)),
            pltpu.SemaphoreType.DMA,
        ],
        compiler_params=params(),
        cost_estimate=cost(2 * members * cells * width * (width + 256), 14 << 20),
        name="forward",
    )(place, in_hbm(grid_input), in_hbm(w_hidden), b_hidden.reshape(1, width), w_out_t)


def score_kernel(pieces, place, target_ref, bias_ref, weight_ref, *refs):
    given, out, (bias, weights_of) = refs[:pieces], refs[pieces:-2], refs[-2:]
    extra, channels, length = given[0].shape
    per = extra - 1
    members = per * pieces
    kappa = ALPHA / (2.0 * members * (members - 1)) + (1.0 - ALPHA) / (2.0 * members * members)
    start = pl.multiple_of(place[0] * length, length)
    bias[...] = jnp.broadcast_to(bias_ref[...], (8, channels)).T
    weights_of[...] = jnp.broadcast_to(weight_ref[...], (8, channels)).T

    def rows_step(i, carry):
        rows = pl.ds(pl.multiple_of(i * 16, 16), 16)
        own = []
        for s in range(pieces):
            base = given[s][0, rows, :].astype(F32)
            own += [base + given[s][1 + m, rows, :].astype(F32) for m in range(per)]
        aim = target_ref[rows, pl.ds(start, length)] - bias[rows, :1]
        weight = weights_of[rows, :1]
        spread = [None] * members
        for j in range(members):
            for k in range(j + 1, members):
                slope = smooth_slope(own[j] - own[k])
                spread[j] = slope if spread[j] is None else spread[j] + slope
                spread[k] = -slope if spread[k] is None else spread[k] - slope
        for j in range(members):
            skill = smooth_slope(own[j] - aim) * (1.0 / members)
            value = weight * (skill - (2.0 * kappa) * spread[j])
            part = j % per
            at = j // per
            while part >= out[at].shape[0]:
                part -= out[at].shape[0]
                at += pieces
            out[at][part, rows, :] = value.astype(BF16)
        return carry

    lax.fori_loop(0, channels // 16, rows_step, 0)


def score(given, target, b_out, channel_weight, place, parts):
    pieces = len(given)
    extra, channels, length = given[0].shape
    shapes = [pltpu.VMEM((part, channels, length), BF16) for part in parts for _ in given]
    return pl.pallas_call(
        functools.partial(score_kernel, pieces),
        in_specs=[ON_SMEM] + [ON_VMEM] * (3 + pieces),
        out_specs=[ON_VMEM] * len(shapes),
        out_shape=shapes,
        scratch_shapes=[pltpu.VMEM((channels, 8), F32)] * 2,
        compiler_params=params(),
        cost_estimate=cost(40_000_000, 1 << 20),
        name="score",
    )(place, target, b_out.reshape(1, channels), channel_weight.reshape(1, channels), *given)


def tiles_kernel(per_region, regions, place, index_ref, tile_ref, w_ref, out_ref, w_t_ref, total):
    blocks, sources, cells, nodes = tile_ref.shape
    total[...] = jnp.zeros_like(total)
    for b in range(blocks):
        for k in range(sources):
            number = index_ref[b, k]
            relative = lax.rem(number // per_region - place[1] + 1 + regions, regions)
            slot = relative * per_region + lax.rem(number, per_region)
            total[slot, b] += tile_ref[b, k].astype(F32).T
    for s in range(total.shape[0]):
        for b in range(blocks):
            out_ref[s * nodes : (s + 1) * nodes, b * cells : (b + 1) * cells] = total[s, b].astype(BF16)
    step = 256
    for lo in range(0, w_ref.shape[0], step):
        w_t_ref[:, lo : lo + step] = w_ref[lo : lo + step, :].T


def tiles_matrix(interp_weight, block_index, w_hidden, place, per_region, regions):
    blocks, _, cells, nodes = interp_weight.shape
    slots = 3 * per_region
    return pl.pallas_call(
        functools.partial(tiles_kernel, per_region, regions),
        in_specs=[ON_SMEM, ON_SMEM, ON_VMEM, ON_VMEM],
        out_specs=[ON_VMEM] * 2,
        out_shape=[
            pltpu.VMEM((slots * nodes, blocks * cells), BF16),
            pltpu.VMEM(w_hidden.shape, BF16),
        ],
        scratch_shapes=[pltpu.VMEM((slots, blocks, nodes, cells), F32)],
        compiler_params=params(),
        cost_estimate=cost(4_000_000, 2 << 20),
        name="tiles",
    )(place, block_index, interp_weight, w_hidden)


def backward_kernel(first, pieces, place, wout_ref, slope_ref, tiles_ref, *refs):
    given = refs[:pieces]
    dpred_ref, dpre_ref, below_ref, own_ref, above_ref = refs[pieces:]
    length = given[0].shape[2]
    members, nodes, width = own_ref.shape
    step = 512
    for m in range(members):
        for s in range(pieces):
            at = lax.rem(place[0] + s, pieces) * length
            rows = pl.ds(pl.multiple_of(at, length), length)
            dpred_ref[m, rows, :] = given[s][m].astype(F32).T.astype(BF16)
        for lo in range(0, width, step):
            cols = slice(lo, lo + step)
            dact = jnp.dot(dpred_ref[m], wout_ref[:, cols], preferred_element_type=F32)
            dpre = (dact * slope_ref[first + m, :, cols].astype(F32)).astype(BF16)
            dpre_ref[m, :, cols] = dpre
            terms = jnp.dot(tiles_ref[...], dpre, preferred_element_type=F32)
            below_ref[m, :, cols] = terms[:nodes].astype(BF16)
            own_ref[m, :, cols] = terms[nodes : 2 * nodes].astype(BF16)
            above_ref[m, :, cols] = terms[2 * nodes :].astype(BF16)


def backward(first, members, given, w_out_t, slope, tiles, place):
    pieces = len(given)
    _, cells, width = slope.shape
    channels = w_out_t.shape[0]
    nodes = tiles.shape[0] // 3
    return pl.pallas_call(
        functools.partial(backward_kernel, first, pieces),
        in_specs=[ON_SMEM] + [ON_VMEM] * (3 + pieces),
        out_specs=[ON_VMEM] * 5,
        out_shape=[
            pltpu.VMEM((members, cells, channels), BF16),
            pltpu.VMEM((members, cells, width), BF16),
            pltpu.VMEM((members, nodes, width), BF16),
            pltpu.VMEM((members, nodes, width), BF16),
            pltpu.VMEM((members, nodes, width), BF16),
        ],
        compiler_params=params(),
        cost_estimate=cost(2 * members * cells * width * (256 + 3 * nodes), 5 << 20),
        name="backward",
    )(place, w_out_t, slope, tiles, *given)


def weights_kernel(turns, groups, cores, place, x_ref, act_ref, *refs):
    parts = (len(refs) - cores) // 2
    dpre = [(ref, m) for ref in refs[:parts] for m in range(ref.shape[0])]
    dpred = [(ref, m) for ref in refs[parts : 2 * parts] for m in range(ref.shape[0])]
    out = refs[2 * parts :]
    width = dpre[0][0].shape[2]
    step = width // groups
    count, rows, _ = out[0].shape
    count //= len(turns)
    across = (((0,), (0,)), ((), ()))
    mine = lax.rem(place[1], cores)
    for i, turn in enumerate(turns):
        at = lax.rem(place[0] + turn, groups) * step
        cols = pl.ds(pl.multiple_of(at, step), step)
        for values, others, wide in (
            (x_ref, dpre, slice(0, width)),
            (act_ref, dpred, slice(width, None)),
        ):
            total = None
            for m, (ref, k) in enumerate(others):
                part = lax.dot_general(values[m, :, cols], ref[k], across, preferred_element_type=F32)
                total = part if total is None else total + part
            total = total.astype(BF16).reshape(count, cores, rows, total.shape[1])
            for b in range(count):
                block = [total[b, c] for c in range(cores)]
                if cores == 1:
                    out[0][i * count + b, :, wide] = block[0]
                else:
                    low = mine == 0
                    out[0][i * count + b, :, wide] = jnp.where(low, block[1], block[0])
                    out[1][i * count + b, :, wide] = jnp.where(low, block[0], block[1])


def weights(x, act, dpre, dpred, place, blocks, groups, cores, turns):
    width = x.shape[2]
    columns = width + dpred[0].shape[2]
    rows = width // blocks
    count = len(turns) * blocks // (groups * cores)
    parts = len(dpre)
    return pl.pallas_call(
        functools.partial(weights_kernel, turns, groups, cores),
        in_specs=[ON_SMEM] + [ON_VMEM] * (2 + 2 * parts),
        out_specs=[ON_VMEM] * cores,
        out_shape=[pltpu.VMEM((count, rows, columns), BF16)] * cores,
        compiler_params=params(),
        cost_estimate=cost(1000, 1000),
        name="weights",
    )(place, x, act, *dpre, *dpred)


def add_kernel(kept_ref, came_ref, *out):
    count = out[0].shape[0]
    for s, ref in enumerate(out):
        for i in range(count):
            at = s * count + i
            ref[i] = (kept_ref[at].astype(F32) + came_ref[at].astype(F32)).astype(BF16)


def add(kept, came, parts):
    blocks, rows, columns = kept.shape
    return pl.pallas_call(
        add_kernel,
        in_specs=[ON_VMEM] * 2,
        out_specs=[ON_VMEM] * parts,
        out_shape=[pltpu.VMEM((blocks // parts, rows, columns), BF16)] * parts,
        compiler_params=params(),
        cost_estimate=cost(1000, 1000),
        name="add",
    )(kept, came)


def split_kernel(which, unit, parts, place, *refs):
    given, out = refs[:-parts], refs[-parts:]
    count = out[0].shape[0]
    mine = lax.rem(place[which] // unit, parts)
    for s in range(parts):
        first = lax.rem(mine + s, parts) * count
        for i in range(count):
            total = given[0][first + i].astype(F32)
            for ref in given[1:]:
                total = total + ref[first + i].astype(F32)
            out[s][i] = total.astype(BF16)


def split(given, place, which, unit, parts):
    blocks, rows, columns = given[0].shape
    return pl.pallas_call(
        functools.partial(split_kernel, which, unit, parts),
        in_specs=[ON_SMEM] + [ON_VMEM] * len(given),
        out_specs=[ON_VMEM] * parts,
        out_shape=[pltpu.VMEM((blocks // parts, rows, columns), BF16)] * parts,
        compiler_params=params(),
        cost_estimate=cost(1000, 1000),
        name="split",
    )(place, *given)


def total_kernel(*refs):
    given, (hidden_ref, output_ref) = refs[:-2], refs[-2:]
    width = hidden_ref.shape[1]
    for ref, cols in ((hidden_ref, slice(0, width)), (output_ref, slice(width, None))):
        total = given[0][0, :, cols].astype(F32)
        for other in given[1:]:
            total = total + other[0, :, cols].astype(F32)
        ref[...] = total


def last_total(given, width):
    _, rows, columns = given[0].shape
    return pl.pallas_call(
        total_kernel,
        in_specs=[ON_VMEM] * len(given),
        out_specs=[ON_VMEM] * 2,
        out_shape=[
            jax.ShapeDtypeStruct((rows, width), F32),
            jax.ShapeDtypeStruct((rows, columns - width), F32),
        ],
        compiler_params=params(),
        cost_estimate=cost(1000, 1000),
        name="total",
    )(*given)


def weight_gradients(x, act, dpre, dpred, place, after):
    groups, regions = lax.axis_size("member"), lax.axis_size("region")
    blocks, width = groups * regions, x.shape[2]
    if regions % 2 or width % (blocks * 16):
        turns = list(range(groups))
        (part,) = weights(x, act, dpre, dpred, place * 0, blocks, groups, 1, turns)
        part = part.reshape(width, -1)
        part = lax.psum_scatter(part, "member", scatter_dimension=0, tiled=True)
        part = lax.psum_scatter(part, "region", scatter_dimension=0, tiled=True).astype(F32)
        return part[:, :width], part[:, width:]
    given = [None] * groups
    for turns in turn_sets(groups):
        away, kept = weights(x, act, dpre, dpred, place, blocks, groups, 2, turns)
        if after is not None:
            (away, kept), _ = lax.optimization_barrier(((away, kept), after))
            after = None
        came = lax.ppermute(away, "region", [(i, i ^ 1) for i in range(regions)])
        for s, part in zip(turns, add(kept, came, len(turns))):
            given[s] = shifted(part, "member", s) if s else part
    chips = regions // 2
    parts = split(given, place, 1, 2, chips)
    given = [parts[0]]
    for s in range(1, chips):
        route = [(i, (i + 2 * s) % regions) for i in range(regions)]
        given.append(lax.ppermute(parts[s], "region", route))
    return last_total(given, width)


def finish_kernel(first, own_ref, up_ref, down_ref, w_ref, *refs):
    out_ref, slots, sems = refs[-3:]
    copies = []
    for m in range(own_ref.shape[0]):
        total = own_ref[m].astype(F32) + up_ref[m].astype(F32) + down_ref[m].astype(F32)
        slots[m] = jnp.dot(total.astype(BF16), w_ref[...], preferred_element_type=F32)
        copies.append(pltpu.make_async_copy(slots.at[m], out_ref.at[first + m], sems.at[m]))
        copies[m].start()
    for copy in copies:
        copy.wait()


def finish(first, members, own, up, down, w_hidden_t, held):
    here, nodes, width = own.shape
    extra = [] if held is None else [held]
    return pl.pallas_call(
        functools.partial(finish_kernel, first),
        in_specs=[ON_VMEM] * 4 + [ANYWHERE] * len(extra),
        out_specs=ANYWHERE,
        out_shape=jax.ShapeDtypeStruct((members, nodes, width), F32),
        scratch_shapes=[pltpu.VMEM(own.shape, F32), pltpu.SemaphoreType.DMA((here,))],
        input_output_aliases={4: 0} if extra else {},
        compiler_params=params(),
        cost_estimate=cost(1000, 1000),
        name="finish",
    )(own, up, down, w_hidden_t, *extra)


def body(
    grid_input, w_hidden, b_hidden, w_out, b_out, target, channel_weight, interp_weight, block_index
):
    members, cells, width = grid_input.shape
    groups, regions = lax.axis_size("member"), lax.axis_size("region")
    per_region = MBLK_REG
    place = jnp.stack([lax.axis_index("member"), lax.axis_index("region")]).astype(jnp.int32)
    w_out_t = w_out.T
    x, w_hidden, act, slope, *sends = forward(grid_input, w_hidden, b_hidden, w_out_t, place, groups)
    tiles, w_hidden_t = tiles_matrix(
        interp_weight, block_index, w_hidden, place, per_region, regions
    )
    given = [sends[0]] + [shifted(sends[s], "member", s) for s in range(1, groups)]
    parts = shares(members)
    adjoint = score(given, target, b_out, channel_weight, place, parts)
    dpred, dpre, own, up, down = [], [], [], [], []
    first = 0
    for i, per in enumerate(parts):
        mine = adjoint[i * groups : (i + 1) * groups]
        back = [mine[0]] + [shifted(mine[s], "member", -s) for s in range(1, groups)]
        one = backward(first, per, back, w_out_t, slope, tiles, place)
        first += per
        dpred.append(one[0])
        dpre.append(one[1])
        own.append(one[3])
        down.append(shifted(one[2], "region", -1))
        up.append(shifted(one[4], "region", 1))
    hidden, output = weight_gradients(x, act, dpre, dpred, place, (up[0], down[0]))
    out = None
    first = 0
    for i, per in enumerate(parts):
        out = finish(first, members, own[i], up[i], down[i], w_hidden_t, out)
        first += per
    return hidden, output, out


def turn_sets(groups):
    return [list(range(groups - 1, 0, -1)), [0]]


def shares(members):
    return [1, 3]


def solution(mesh):
    placed = (
        P("member", "region", None),
        P(),
        P(),
        P(),
        P(),
        P(None, "region"),
        P(),
        P("region", None, None, None),
        P("region", None),
    )
    return jax.shard_map(
        body,
        mesh=mesh,
        in_specs=placed,
        out_specs=(
            P(("member", "region"), None),
            P(("member", "region"), None),
            P("member", "region", None),
        ),
        check_vma=False,
    )
```

```python
import functools

import jax
import jax.numpy as jnp
from jax import lax
from jax.experimental import pallas as pl
from jax.experimental.pallas import tpu as pltpu
from jax.sharding import PartitionSpec as P

ALPHA = 0.95
SMOOTH = 0.25
MBLK_REG = 2
SCOPED = 16 * 1024 * 1024
F32 = jnp.float32
BF16 = jnp.bfloat16
ON_VMEM = pl.BlockSpec(memory_space=pltpu.VMEM)
ON_HBM = pl.BlockSpec(memory_space=pltpu.HBM)
ON_SMEM = pl.BlockSpec(memory_space=pltpu.SMEM)
ANYWHERE = pl.BlockSpec(memory_space=pl.ANY)


def shifted(block, axis, distance):
    count = lax.axis_size(axis)
    return lax.ppermute(block, axis, [((i - distance) % count, i) for i in range(count)])


def exchanged(block, axis, bit):
    count = lax.axis_size(axis)
    return lax.ppermute(block, axis, [(i, i ^ bit) for i in range(count)])


def smooth_slope(diff):
    return diff * lax.rsqrt(diff * diff + SMOOTH * SMOOTH)


def params():
    return pltpu.CompilerParams(vmem_limit_bytes=SCOPED)


def in_hbm(array):
    return pltpu.with_memory_space_constraint(array, pltpu.HBM)


def cost(flops, moved):
    return pl.CostEstimate(flops=int(flops), bytes_accessed=int(moved), transcendentals=0)


def cells_forward(turn, place, pieces, x_ref, w_ref, b_ref, wout_ref, act_ref, slope_ref, send_ref):
    members, cells, width = x_ref.shape
    length = cells // pieces
    at = lax.rem(place[0] + turn, pieces) * length
    x = x_ref[:, pl.ds(pl.multiple_of(at, length), length), :].reshape(members * length, width)
    each = 2 if members % 2 == 0 else 1
    base = None
    for m in range(0, members, each):
        rows = x[m * length : (m + each) * length]
        pre = jnp.dot(rows, w_ref[...], preferred_element_type=F32) + b_ref[...]
        logistic = 0.5 * jnp.tanh(0.5 * pre) + 0.5
        act = pre * logistic
        slope = (logistic + act * (1.0 - logistic)).astype(BF16)
        slope_ref[m : m + each] = slope.reshape(each, length, width)
        act = act.astype(BF16)
        act_ref[m : m + each] = act.reshape(each, length, width)
        line = lax.dot_general(
            wout_ref[...], act, (((1,), (1,)), ((), ())), preferred_element_type=F32
        )
        if m == 0:
            first = line[:, :length].astype(BF16)
            send_ref[0] = first
            base = first.astype(F32)
        for i in range(each):
            send_ref[1 + m + i] = (line[:, i * length : (i + 1) * length] - base).astype(BF16)


def first_kernel(
    turn, pieces, place, x_hbm, w_hbm, b_hbm, wout_hbm, x_ref, w_ref, b_ref, wout_ref,
    act_ref, slope_ref, send_ref, x_sems, sems
):
    length = x_ref.shape[1] // pieces
    x_copies = []
    for s in range(pieces):
        at = lax.rem(place[0] + turn + s, pieces) * length
        cells = pl.ds(pl.multiple_of(at, length), length)
        x_copies.append(
            pltpu.make_async_copy(x_hbm.at[:, cells, :], x_ref.at[:, cells, :], x_sems.at[s])
        )
    copies = [
        pltpu.make_async_copy(b_hbm, b_ref, sems.at[0]),
        pltpu.make_async_copy(w_hbm, w_ref, sems.at[1]),
        pltpu.make_async_copy(wout_hbm, wout_ref, sems.at[2]),
    ]
    for copy in copies[:2] + x_copies[:1] + copies[2:]:
        copy.start()
    for copy in copies + x_copies[:1]:
        copy.wait()
    for copy in x_copies[1:]:
        copy.start()
    cells_forward(turn, place, pieces, x_ref, w_ref, b_ref, wout_ref, act_ref, slope_ref, send_ref)
    for copy in x_copies[1:]:
        copy.wait()


def later_kernel(turn, pieces, place, x_ref, w_ref, b_ref, wout_ref, act_ref, slope_ref, send_ref):
    cells_forward(turn, place, pieces, x_ref, w_ref, b_ref, wout_ref, act_ref, slope_ref, send_ref)


def forward(grid_input, w_hidden, b_hidden, w_out_t, place, pieces):
    members, cells, width = grid_input.shape
    channels = w_out_t.shape[0]
    length = cells // pieces
    rows = pltpu.VMEM((members, length, width), BF16)
    results = [rows, rows, pltpu.VMEM((members + 1, channels, length), BF16)]
    turns = far_first(pieces)
    estimate = cost(1000, 1000)
    x, w, b, w_out, *one = pl.pallas_call(
        functools.partial(first_kernel, turns[0], pieces),
        in_specs=[ON_SMEM] + [ON_HBM] * 4,
        out_specs=[ON_VMEM] * 7,
        out_shape=[
            pltpu.VMEM(grid_input.shape, BF16),
            pltpu.VMEM(w_hidden.shape, BF16),
            pltpu.VMEM((1, width), F32),
            pltpu.VMEM(w_out_t.shape, BF16),
        ]
        + results,
        scratch_shapes=[pltpu.SemaphoreType.DMA((pieces,)), pltpu.SemaphoreType.DMA((3,))],
        compiler_params=params(),
        cost_estimate=estimate,
        name="forward",
    )(place, in_hbm(grid_input), in_hbm(w_hidden), in_hbm(b_hidden.reshape(1, width)), in_hbm(w_out_t))
    done = {turns[0]: one}
    for turn in turns[1:]:
        b, _ = lax.optimization_barrier((b, one[2]))
        one = pl.pallas_call(
            functools.partial(later_kernel, turn, pieces),
            in_specs=[ON_SMEM] + [ON_VMEM] * 4,
            out_specs=[ON_VMEM] * 3,
            out_shape=results,
            compiler_params=params(),
            cost_estimate=estimate,
            name="forward",
        )(place, x, w, b, w_out)
        done[turn] = one
    act, slope, sends = zip(*(done[s] for s in range(pieces)))
    return x, w, w_out, list(act), list(slope), list(sends)


def far_first(pieces):
    return sorted(range(pieces), key=lambda s: (s == 0, -min(s, pieces - s), s))


def score_kernel(pieces, place, target_ref, bias_ref, weight_ref, *refs):
    given, out, (bias, weights_of) = refs[:pieces], refs[pieces:-2], refs[-2:]
    extra, channels, length = given[0].shape
    per = extra - 1
    members = per * pieces
    kappa = ALPHA / (2.0 * members * (members - 1)) + (1.0 - ALPHA) / (2.0 * members * members)
    start = pl.multiple_of(place[0] * length, length)
    bias[...] = jnp.broadcast_to(bias_ref[...], (8, channels)).T
    weights_of[...] = jnp.broadcast_to(weight_ref[...], (8, channels)).T

    def rows_step(i, carry):
        rows = pl.ds(pl.multiple_of(i * 16, 16), 16)
        own = []
        for s in range(pieces):
            base = given[s][0, rows, :].astype(F32)
            own += [base + given[s][m, rows, :].astype(F32) for m in range(1, extra)]
        aim = target_ref[rows, pl.ds(start, length)] - bias[rows, :1]
        weight = weights_of[rows, :1]
        spread = [None] * members
        for j in range(members):
            for k in range(j + 1, members):
                slope = smooth_slope(own[j] - own[k])
                spread[j] = slope if spread[j] is None else spread[j] + slope
                spread[k] = -slope if spread[k] is None else spread[k] - slope
        for j in range(members):
            skill = smooth_slope(own[j] - aim) * (1.0 / members)
            value = weight * (skill - (2.0 * kappa) * spread[j])
            part = j % per
            at = j // per
            while part >= out[at].shape[0]:
                part -= out[at].shape[0]
                at += pieces
            out[at][part, rows, :] = value.astype(BF16)
        return carry

    lax.fori_loop(0, channels // 16, rows_step, 0)


def score(given, target, b_out, channel_weight, place, parts):
    pieces = len(given)
    extra, channels, length = given[0].shape
    shapes = [pltpu.VMEM((part, channels, length), BF16) for part in parts for _ in given]
    return pl.pallas_call(
        functools.partial(score_kernel, pieces),
        in_specs=[ON_SMEM] + [ON_VMEM] * (3 + pieces),
        out_specs=[ON_VMEM] * len(shapes),
        out_shape=shapes,
        scratch_shapes=[pltpu.VMEM((channels, 8), F32)] * 2,
        compiler_params=params(),
        cost_estimate=cost(40_000_000, 1 << 20),
        name="score",
    )(place, target, b_out.reshape(1, channels), channel_weight.reshape(1, channels), *given)


def tiles_kernel(per_region, regions, place, index_ref, tile_ref, w_ref, out_ref, w_t_ref, total):
    blocks, sources, cells, nodes = tile_ref.shape
    total[...] = jnp.zeros_like(total)
    for b in range(blocks):
        for k in range(sources):
            number = index_ref[b, k]
            relative = lax.rem(number // per_region - place[1] + 1 + regions, regions)
            slot = relative * per_region + lax.rem(number, per_region)
            total[slot, b] += tile_ref[b, k].astype(F32).T
    for s in range(total.shape[0]):
        for b in range(blocks):
            out_ref[s * nodes : (s + 1) * nodes, b * cells : (b + 1) * cells] = total[s, b].astype(BF16)
    step = 256
    for lo in range(0, w_ref.shape[0], step):
        w_t_ref[:, lo : lo + step] = w_ref[lo : lo + step, :].T


def tiles_matrix(interp_weight, block_index, w_hidden, place, per_region, regions):
    blocks, _, cells, nodes = interp_weight.shape
    slots = 3 * per_region
    return pl.pallas_call(
        functools.partial(tiles_kernel, per_region, regions),
        in_specs=[ON_SMEM, ON_SMEM, ON_VMEM, ON_VMEM],
        out_specs=[ON_VMEM] * 2,
        out_shape=[
            pltpu.VMEM((slots * nodes, blocks * cells), BF16),
            pltpu.VMEM(w_hidden.shape, BF16),
        ],
        scratch_shapes=[pltpu.VMEM((slots, blocks, nodes, cells), F32)],
        compiler_params=params(),
        cost_estimate=cost(4_000_000, 2 << 20),
        name="tiles",
    )(place, block_index, interp_weight, w_hidden)


def backward_kernel(first, pieces, place, wout_ref, tiles_ref, *refs):
    given, slopes = refs[:pieces], refs[pieces : 2 * pieces]
    dpred_ref, dpre_ref, below_ref, own_ref, above_ref = refs[2 * pieces :]
    length = given[0].shape[2]
    members, nodes, width = own_ref.shape
    step = 512
    for m in range(members):
        for s in range(pieces):
            rows = slice(s * length, (s + 1) * length)
            dpred_ref[m, rows, :] = given[s][m].astype(F32).T.astype(BF16)
        for lo in range(0, width, step):
            cols = slice(lo, lo + step)
            dact = jnp.dot(dpred_ref[m], wout_ref[:, cols], preferred_element_type=F32)
            for s in range(pieces):
                slope = slopes[s][first + m, :, cols].astype(F32)
                dpre = (dact[s * length : (s + 1) * length] * slope).astype(BF16)
                at = lax.rem(place[0] + s, pieces) * length
                dpre_ref[m, pl.ds(pl.multiple_of(at, length), length), cols] = dpre
            terms = jnp.dot(tiles_ref[...], dpre_ref[m, :, cols], preferred_element_type=F32)
            below_ref[m, :, cols] = terms[:nodes].astype(BF16)
            own_ref[m, :, cols] = terms[nodes : 2 * nodes].astype(BF16)
            above_ref[m, :, cols] = terms[2 * nodes :].astype(BF16)


def backward(first, members, given, w_out_t, slope, tiles, place):
    pieces = len(given)
    _, length, width = slope[0].shape
    cells = length * pieces
    channels = w_out_t.shape[0]
    nodes = tiles.shape[0] // 3
    return pl.pallas_call(
        functools.partial(backward_kernel, first, pieces),
        in_specs=[ON_SMEM] + [ON_VMEM] * (2 + pieces + len(slope)),
        out_specs=[ON_VMEM] * 5,
        out_shape=[
            pltpu.VMEM((members, cells, channels), BF16),
            pltpu.VMEM((members, cells, width), BF16),
            pltpu.VMEM((members, nodes, width), BF16),
            pltpu.VMEM((members, nodes, width), BF16),
            pltpu.VMEM((members, nodes, width), BF16),
        ],
        compiler_params=params(),
        cost_estimate=cost(2 * members * cells * width * (256 + 3 * nodes), 5 << 20),
        name="backward",
    )(place, w_out_t, tiles, *given, *slope)


def weights_kernel(turns, groups, cores, counts, place, *refs):
    split_at, lists = 0, []
    for count in counts:
        some = refs[split_at : split_at + count]
        lists.append([ref.at[m] for ref in some for m in range(ref.shape[0])])
        split_at += count
    x, act, dpre, dpred = lists
    act = [act[m :: len(x)] for m in range(len(x))]
    out = refs[split_at:]
    width = dpre[0].shape[1]
    step = width // groups
    count, rows, _ = out[0].shape
    count //= len(turns)
    across = (((0,), (0,)), ((), ()))
    mine = lax.rem(place[1], cores)
    for i, turn in enumerate(turns):
        at = lax.rem(place[0] + turn, groups) * step
        cols = pl.ds(pl.multiple_of(at, step), step)
        for values, others, wide in (
            (x, dpre, slice(0, width)),
            (act, dpred, slice(width, None)),
        ):
            total = None
            for value, other in zip(values, others):
                if isinstance(value, list):
                    value = jnp.concatenate([piece[:, cols] for piece in value], axis=0)
                else:
                    value = value[:, cols]
                part = lax.dot_general(value, other[...], across, preferred_element_type=F32)
                total = part if total is None else total + part
            total = total.astype(BF16).reshape(count, cores, rows, total.shape[1])
            for b in range(count):
                block = [total[b, c] for c in range(cores)]
                if cores == 1:
                    out[0][i * count + b, :, wide] = block[0]
                else:
                    low = mine == 0
                    out[0][i * count + b, :, wide] = jnp.where(low, block[1], block[0])
                    out[1][i * count + b, :, wide] = jnp.where(low, block[0], block[1])


def weights(x, act, dpre, dpred, place, blocks, groups, cores, turns):
    width = x[0].shape[2]
    columns = width + dpred[0].shape[2]
    rows = width // blocks
    count = len(turns) * blocks // (groups * cores)
    counts = [len(x), len(act), len(dpre), len(dpred)]
    return pl.pallas_call(
        functools.partial(weights_kernel, turns, groups, cores, counts),
        in_specs=[ON_SMEM] + [ON_VMEM] * sum(counts),
        out_specs=[ON_VMEM] * cores,
        out_shape=[pltpu.VMEM((count, rows, columns), BF16)] * cores,
        compiler_params=params(),
        cost_estimate=cost(1000, 1000),
        name="weights",
    )(place, *x, *act, *dpre, *dpred)


def add_kernel(kept_ref, came_ref, *out):
    count = out[0].shape[0]
    for s, ref in enumerate(out):
        for i in range(count):
            at = s * count + i
            ref[i] = (kept_ref[at].astype(F32) + came_ref[at].astype(F32)).astype(BF16)


def add(kept, came, parts):
    blocks, rows, columns = kept.shape
    return pl.pallas_call(
        add_kernel,
        in_specs=[ON_VMEM] * 2,
        out_specs=[ON_VMEM] * parts,
        out_shape=[pltpu.VMEM((blocks // parts, rows, columns), BF16)] * parts,
        compiler_params=params(),
        cost_estimate=cost(1000, 1000),
        name="add",
    )(kept, came)


def split_kernel(which, unit, parts, place, *refs):
    given, out = refs[:-parts], refs[-parts:]
    count = out[0].shape[0]
    mine = lax.rem(place[which] // unit, parts)
    for s in range(parts):
        first = lax.rem(mine + s, parts) * count
        for i in range(count):
            total = given[0][first + i].astype(F32)
            for ref in given[1:]:
                total = total + ref[first + i].astype(F32)
            out[s][i] = total.astype(BF16)


def split(given, place, which, unit, parts):
    blocks, rows, columns = given[0].shape
    return pl.pallas_call(
        functools.partial(split_kernel, which, unit, parts),
        in_specs=[ON_SMEM] + [ON_VMEM] * len(given),
        out_specs=[ON_VMEM] * parts,
        out_shape=[pltpu.VMEM((blocks // parts, rows, columns), BF16)] * parts,
        compiler_params=params(),
        cost_estimate=cost(1000, 1000),
        name="split",
    )(place, *given)


def total_kernel(*refs):
    given, (hidden_ref, output_ref) = refs[:-2], refs[-2:]
    width = hidden_ref.shape[1]
    for ref, cols in ((hidden_ref, slice(0, width)), (output_ref, slice(width, None))):
        total = given[0][0, :, cols].astype(F32)
        for other in given[1:]:
            total = total + other[0, :, cols].astype(F32)
        ref[...] = total


def last_total(given, width):
    _, rows, columns = given[0].shape
    return pl.pallas_call(
        total_kernel,
        in_specs=[ON_VMEM] * len(given),
        out_specs=[ON_VMEM] * 2,
        out_shape=[
            jax.ShapeDtypeStruct((rows, width), F32),
            jax.ShapeDtypeStruct((rows, columns - width), F32),
        ],
        compiler_params=params(),
        cost_estimate=cost(1000, 1000),
        name="total",
    )(*given)


def weight_gradients(x, act, dpre, dpred, place, after, done):
    groups, regions = lax.axis_size("member"), lax.axis_size("region")
    blocks, width = groups * regions, x[0].shape[2]
    if regions % 2 or width % (blocks * 16):
        turns = list(range(groups))
        (part,) = weights(x, act, dpre, dpred, place * 0, blocks, groups, 1, turns)
        part = part.reshape(width, -1)
        part = lax.psum_scatter(part, "member", scatter_dimension=0, tiled=True)
        part = lax.psum_scatter(part, "region", scatter_dimension=0, tiled=True).astype(F32)
        return part[:, :width], part[:, width:], done
    given = [None] * groups
    for turns in turn_sets(groups):
        away, kept = weights(x, act, dpre, dpred, place, blocks, groups, 2, turns)
        if after is not None:
            (away, kept), _ = lax.optimization_barrier(((away, kept), after))
            after = None
        came = lax.ppermute(away, "region", [(i, i ^ 1) for i in range(regions)])
        for s, part in zip(turns, add(kept, came, len(turns))):
            given[s] = shifted(part, "member", s) if s else part
    given, done = lax.optimization_barrier((given, done))
    chips = regions // 2
    parts = split(given, place, 1, 2, chips)
    given = [parts[0]]
    for s in range(1, chips):
        route = [(i, (i + 2 * s) % regions) for i in range(regions)]
        given.append(lax.ppermute(parts[s], "region", route))
    return *last_total(given, width), done


def finish_kernel(first, own_ref, up_ref, down_ref, w_ref, *refs):
    out_ref, slots, sems = refs[-3:]
    copies = []
    for m in range(own_ref.shape[0]):
        total = own_ref[m].astype(F32) + up_ref[m].astype(F32) + down_ref[m].astype(F32)
        slots[m] = jnp.dot(total.astype(BF16), w_ref[...], preferred_element_type=F32)
        copies.append(pltpu.make_async_copy(slots.at[m], out_ref.at[first + m], sems.at[m]))
        copies[m].start()
    for copy in copies:
        copy.wait()


def finish(first, members, own, up, down, w_hidden_t, held):
    here, nodes, width = own.shape
    extra = [] if held is None else [held]
    return pl.pallas_call(
        functools.partial(finish_kernel, first),
        in_specs=[ON_VMEM] * 4 + [ANYWHERE] * len(extra),
        out_specs=ANYWHERE,
        out_shape=jax.ShapeDtypeStruct((members, nodes, width), F32),
        scratch_shapes=[pltpu.VMEM(own.shape, F32), pltpu.SemaphoreType.DMA((here,))],
        input_output_aliases={4: 0} if extra else {},
        compiler_params=params(),
        cost_estimate=cost(1000, 1000),
        name="finish",
    )(own, up, down, w_hidden_t, *extra)


def body(
    grid_input, w_hidden, b_hidden, w_out, b_out, target, channel_weight, interp_weight, block_index
):
    members, cells, width = grid_input.shape
    groups, regions = lax.axis_size("member"), lax.axis_size("region")
    per_region = MBLK_REG
    place = jnp.stack([lax.axis_index("member"), lax.axis_index("region")]).astype(jnp.int32)
    w_out_t = w_out.T
    x, w_hidden, w_out_t, act, slope, sends = forward(
        grid_input, w_hidden, b_hidden, w_out_t, place, groups
    )
    tiles, w_hidden_t = tiles_matrix(
        interp_weight, block_index, w_hidden, place, per_region, regions
    )
    x = [x]
    given = [sends[0]] + [shifted(sends[s], "member", s) for s in range(1, groups)]
    parts = shares(members)
    adjoint = score(given, target, b_out, channel_weight, place, parts)
    dpred, dpre, own, up, down = [], [], [], [], []
    first = 0
    for i, per in enumerate(parts):
        mine = adjoint[i * groups : (i + 1) * groups]
        back = [mine[0]] + [shifted(mine[s], "member", -s) for s in range(1, groups)]
        if dpred:
            back, _ = lax.optimization_barrier((back, dpred[-1]))
        one = backward(first, per, back, w_out_t, slope, tiles, place)
        first += per
        dpred.append(one[0])
        dpre.append(one[1])
        own.append(one[3])
        down.append(shifted(one[2], "region", -1))
        up.append(shifted(one[4], "region", 1))
    out = finish(0, members, own[0], up[0], down[0], w_hidden_t, None)
    hidden, output, out = weight_gradients(x, act, dpre, dpred, place, (up[0], down[0]), out)
    first = parts[0]
    for i, per in list(enumerate(parts))[1:]:
        out = finish(first, members, own[i], up[i], down[i], w_hidden_t, out)
        first += per
    return hidden, output, out


def turn_sets(groups):
    return [list(range(groups - 1, 0, -1)), [0]]


def shares(members):
    return [1, 3]


def solution(mesh):
    placed = (
        P("member", "region", None),
        P(),
        P(),
        P(),
        P(),
        P(None, "region"),
        P(),
        P("region", None, None, None),
        P("region", None),
    )
    return jax.shard_map(
        body,
        mesh=mesh,
        in_specs=placed,
        out_specs=(
            P(("member", "region"), None),
            P(("member", "region"), None),
            P("member", "region", None),
        ),
        check_vma=False,
    )
```

```python
import functools

import jax
import jax.numpy as jnp
from jax import lax
from jax.experimental import pallas as pl
from jax.experimental.pallas import tpu as pltpu
from jax.sharding import PartitionSpec as P

ALPHA = 0.95
SMOOTH = 0.25
MBLK_REG = 2
SCOPED = 16 * 1024 * 1024
F32 = jnp.float32
BF16 = jnp.bfloat16
ON_VMEM = pl.BlockSpec(memory_space=pltpu.VMEM)
ON_HBM = pl.BlockSpec(memory_space=pltpu.HBM)
ON_SMEM = pl.BlockSpec(memory_space=pltpu.SMEM)
ANYWHERE = pl.BlockSpec(memory_space=pl.ANY)


def shifted(block, axis, distance):
    count = lax.axis_size(axis)
    return lax.ppermute(block, axis, [((i - distance) % count, i) for i in range(count)])


def exchanged(block, axis, bit):
    count = lax.axis_size(axis)
    return lax.ppermute(block, axis, [(i, i ^ bit) for i in range(count)])


def smooth_slope(diff):
    return diff * lax.rsqrt(diff * diff + SMOOTH * SMOOTH)


def params():
    return pltpu.CompilerParams(vmem_limit_bytes=SCOPED)


def in_hbm(array):
    return pltpu.with_memory_space_constraint(array, pltpu.HBM)


def cost(flops, moved):
    return pl.CostEstimate(flops=int(flops), bytes_accessed=int(moved), transcendentals=0)


def cells_forward(turn, place, pieces, x_ref, w_ref, b_ref, wout_ref, act_ref, slope_ref, send_ref):
    members, cells, width = x_ref.shape
    length = cells // pieces
    at = lax.rem(place[0] + turn, pieces) * length
    x = x_ref[:, pl.ds(pl.multiple_of(at, length), length), :].reshape(members * length, width)
    each = 2 if members % 2 == 0 else 1
    base = None
    for m in range(0, members, each):
        rows = x[m * length : (m + each) * length]
        pre = jnp.dot(rows, w_ref[...], preferred_element_type=F32) + b_ref[...]
        logistic = 0.5 * jnp.tanh(0.5 * pre) + 0.5
        act = pre * logistic
        slope = (logistic + act * (1.0 - logistic)).astype(BF16)
        slope_ref[m : m + each] = slope.reshape(each, length, width)
        act = act.astype(BF16)
        act_ref[m : m + each] = act.reshape(each, length, width)
        line = lax.dot_general(
            wout_ref[...], act, (((1,), (1,)), ((), ())), preferred_element_type=F32
        )
        if m == 0:
            first = line[:, :length].astype(BF16)
            send_ref[0] = first
            base = first.astype(F32)
        for i in range(each):
            send_ref[1 + m + i] = (line[:, i * length : (i + 1) * length] - base).astype(BF16)


def first_kernel(
    turn, pieces, place, x_hbm, w_hbm, b_hbm, wout_hbm, x_ref, w_ref, b_ref, wout_ref,
    act_ref, slope_ref, send_ref, x_sems, sems
):
    length = x_ref.shape[1] // pieces
    x_copies = []
    for s in range(pieces):
        at = lax.rem(place[0] + turn + s, pieces) * length
        cells = pl.ds(pl.multiple_of(at, length), length)
        x_copies.append(
            pltpu.make_async_copy(x_hbm.at[:, cells, :], x_ref.at[:, cells, :], x_sems.at[s])
        )
    copies = [
        pltpu.make_async_copy(b_hbm, b_ref, sems.at[0]),
        pltpu.make_async_copy(w_hbm, w_ref, sems.at[1]),
        pltpu.make_async_copy(wout_hbm, wout_ref, sems.at[2]),
    ]
    for copy in copies[:2] + x_copies[:1] + copies[2:]:
        copy.start()
    for copy in copies + x_copies[:1]:
        copy.wait()
    for copy in x_copies[1:]:
        copy.start()
    cells_forward(turn, place, pieces, x_ref, w_ref, b_ref, wout_ref, act_ref, slope_ref, send_ref)
    for copy in x_copies[1:]:
        copy.wait()


def later_kernel(turn, pieces, place, x_ref, w_ref, b_ref, wout_ref, act_ref, slope_ref, send_ref):
    cells_forward(turn, place, pieces, x_ref, w_ref, b_ref, wout_ref, act_ref, slope_ref, send_ref)


def forward(grid_input, w_hidden, b_hidden, w_out_t, place, pieces):
    members, cells, width = grid_input.shape
    channels = w_out_t.shape[0]
    length = cells // pieces
    rows = pltpu.VMEM((members, length, width), BF16)
    results = [rows, rows, pltpu.VMEM((members + 1, channels, length), BF16)]
    turns = far_first(pieces)
    estimate = cost(1000, 1000)
    x, w, b, w_out, *one = pl.pallas_call(
        functools.partial(first_kernel, turns[0], pieces),
        in_specs=[ON_SMEM] + [ON_HBM] * 4,
        out_specs=[ON_VMEM] * 7,
        out_shape=[
            pltpu.VMEM(grid_input.shape, BF16),
            pltpu.VMEM(w_hidden.shape, BF16),
            pltpu.VMEM((1, width), F32),
            pltpu.VMEM(w_out_t.shape, BF16),
        ]
        + results,
        scratch_shapes=[pltpu.SemaphoreType.DMA((pieces,)), pltpu.SemaphoreType.DMA((3,))],
        compiler_params=params(),
        cost_estimate=estimate,
        name="forward",
    )(place, in_hbm(grid_input), in_hbm(w_hidden), in_hbm(b_hidden.reshape(1, width)), in_hbm(w_out_t))
    done = {turns[0]: one}
    for turn in turns[1:]:
        b, _ = lax.optimization_barrier((b, one[2]))
        one = pl.pallas_call(
            functools.partial(later_kernel, turn, pieces),
            in_specs=[ON_SMEM] + [ON_VMEM] * 4,
            out_specs=[ON_VMEM] * 3,
            out_shape=results,
            compiler_params=params(),
            cost_estimate=estimate,
            name="forward",
        )(place, x, w, b, w_out)
        done[turn] = one
    act, slope, sends = zip(*(done[s] for s in range(pieces)))
    return x, w, w_out, list(act), list(slope), list(sends)


def far_first(pieces):
    return sorted(range(pieces), key=lambda s: (s == 0, -min(s, pieces - s), s))


def score_kernel(pieces, place, target_ref, bias_ref, weight_ref, *refs):
    given, out, (bias, weights_of) = refs[:pieces], refs[pieces:-2], refs[-2:]
    extra, channels, length = given[0].shape
    per = extra - 1
    members = per * pieces
    kappa = ALPHA / (2.0 * members * (members - 1)) + (1.0 - ALPHA) / (2.0 * members * members)
    start = pl.multiple_of(place[0] * length, length)
    bias[...] = jnp.broadcast_to(bias_ref[...], (8, channels)).T
    weights_of[...] = jnp.broadcast_to(weight_ref[...], (8, channels)).T

    def rows_step(i, carry):
        rows = pl.ds(pl.multiple_of(i * 16, 16), 16)
        own = []
        for s in range(pieces):
            base = given[s][0, rows, :].astype(F32)
            own += [base + given[s][m, rows, :].astype(F32) for m in range(1, extra)]
        aim = target_ref[rows, pl.ds(start, length)] - bias[rows, :1]
        weight = weights_of[rows, :1]
        halves = []
        for half in (slice(0, 8), slice(8, 16)):
            mine = [value[half] for value in own]
            spread = [None] * members
            for j in range(members):
                for k in range(j + 1, members):
                    slope = smooth_slope(mine[j] - mine[k])
                    spread[j] = slope if spread[j] is None else spread[j] + slope
                    spread[k] = -slope if spread[k] is None else spread[k] - slope
            skill = [smooth_slope(value - aim[half]) * (1.0 / members) for value in mine]
            halves.append(
                [weight[half] * (a - (2.0 * kappa) * b) for a, b in zip(skill, spread)]
            )
        for j in range(members):
            part = j % per
            at = j // per
            while part >= out[at].shape[0]:
                part -= out[at].shape[0]
                at += pieces
            value = jnp.concatenate([half[j] for half in halves], axis=0)
            out[at][part, rows, :] = value.astype(BF16)
        return carry

    lax.fori_loop(0, channels // 16, rows_step, 0)


def score(given, target, b_out, channel_weight, place, parts):
    pieces = len(given)
    extra, channels, length = given[0].shape
    shapes = [pltpu.VMEM((part, channels, length), BF16) for part in parts for _ in given]
    return pl.pallas_call(
        functools.partial(score_kernel, pieces),
        in_specs=[ON_SMEM] + [ON_VMEM] * (3 + pieces),
        out_specs=[ON_VMEM] * len(shapes),
        out_shape=shapes,
        scratch_shapes=[pltpu.VMEM((channels, 8), F32)] * 2,
        compiler_params=params(),
        cost_estimate=cost(40_000_000, 1 << 20),
        name="score",
    )(place, target, b_out.reshape(1, channels), channel_weight.reshape(1, channels), *given)


def tiles_kernel(per_region, regions, place, index_ref, tile_ref, w_ref, out_ref, own_ref, w_t_ref, total):
    blocks, sources, cells, nodes = tile_ref.shape
    total[...] = jnp.zeros_like(total)
    for b in range(blocks):
        for k in range(sources):
            number = index_ref[b, k]
            relative = lax.rem(number // per_region - place[1] + 1 + regions, regions)
            slot = relative * per_region + lax.rem(number, per_region)
            total[slot, b] += tile_ref[b, k].astype(F32).T
    for s in range(total.shape[0]):
        ref, to = (own_ref, s - per_region) if s // per_region == 1 else (out_ref, s if s < per_region else s - per_region)
        for b in range(blocks):
            ref[to * nodes : (to + 1) * nodes, b * cells : (b + 1) * cells] = total[s, b].astype(BF16)
    step = 256
    for lo in range(0, w_ref.shape[0], step):
        w_t_ref[:, lo : lo + step] = w_ref[lo : lo + step, :].T


def tiles_matrix(interp_weight, block_index, w_hidden, place, per_region, regions):
    blocks, _, cells, nodes = interp_weight.shape
    slots = 3 * per_region
    return pl.pallas_call(
        functools.partial(tiles_kernel, per_region, regions),
        in_specs=[ON_SMEM, ON_SMEM, ON_VMEM, ON_VMEM],
        out_specs=[ON_VMEM] * 3,
        out_shape=[
            pltpu.VMEM((2 * per_region * nodes, blocks * cells), BF16),
            pltpu.VMEM((per_region * nodes, blocks * cells), BF16),
            pltpu.VMEM(w_hidden.shape, BF16),
        ],
        scratch_shapes=[pltpu.VMEM((slots, blocks, nodes, cells), F32)],
        compiler_params=params(),
        cost_estimate=cost(4_000_000, 2 << 20),
        name="tiles",
    )(place, block_index, interp_weight, w_hidden)


def backward_kernel(first, pieces, place, wout_ref, tiles_ref, *refs):
    given, slopes = refs[:pieces], refs[pieces : 2 * pieces]
    dpred_ref, dpre_ref, below_ref, above_ref = refs[2 * pieces :]
    length = given[0].shape[2]
    members, nodes, width = below_ref.shape
    step = 512
    for m in range(members):
        for s in range(pieces):
            rows = slice(s * length, (s + 1) * length)
            dpred_ref[m, rows, :] = given[s][m].astype(F32).T.astype(BF16)
        for lo in range(0, width, step):
            cols = slice(lo, lo + step)
            dact = jnp.dot(dpred_ref[m], wout_ref[:, cols], preferred_element_type=F32)
            for s in range(pieces):
                slope = slopes[s][first + m, :, cols].astype(F32)
                dpre = (dact[s * length : (s + 1) * length] * slope).astype(BF16)
                at = lax.rem(place[0] + s, pieces) * length
                dpre_ref[m, pl.ds(pl.multiple_of(at, length), length), cols] = dpre
            terms = jnp.dot(tiles_ref[...], dpre_ref[m, :, cols], preferred_element_type=F32)
            below_ref[m, :, cols] = terms[:nodes].astype(BF16)
            above_ref[m, :, cols] = terms[nodes:].astype(BF16)


def backward(first, members, given, w_out_t, slope, tiles, place):
    pieces = len(given)
    _, length, width = slope[0].shape
    cells = length * pieces
    channels = w_out_t.shape[0]
    nodes = tiles.shape[0] // 2
    return pl.pallas_call(
        functools.partial(backward_kernel, first, pieces),
        in_specs=[ON_SMEM] + [ON_VMEM] * (2 + pieces + len(slope)),
        out_specs=[ON_VMEM] * 4,
        out_shape=[
            pltpu.VMEM((members, cells, channels), BF16),
            pltpu.VMEM((members, cells, width), BF16),
            pltpu.VMEM((members, nodes, width), BF16),
            pltpu.VMEM((members, nodes, width), BF16),
        ],
        compiler_params=params(),
        cost_estimate=cost(2 * members * cells * width * (256 + 3 * nodes), 5 << 20),
        name="backward",
    )(place, w_out_t, tiles, *given, *slope)


def own_kernel(tiles_ref, dpre_ref, out_ref):
    for m in range(dpre_ref.shape[0]):
        out_ref[m] = jnp.dot(tiles_ref[...], dpre_ref[m], preferred_element_type=F32)


def own_terms(tiles, dpre):
    members, cells, width = dpre.shape
    return pl.pallas_call(
        own_kernel,
        in_specs=[ON_VMEM] * 2,
        out_specs=ON_VMEM,
        out_shape=pltpu.VMEM((members, tiles.shape[0], width), F32),
        compiler_params=params(),
        cost_estimate=cost(1000, 1000),
        name="own",
    )(tiles, dpre)


def weights_kernel(turns, groups, cores, counts, place, *refs):
    split_at, lists = 0, []
    for count in counts:
        lists.append(refs[split_at : split_at + count])
        split_at += count
    (x,), acts, dpre, dpred = lists
    out = refs[split_at:]
    width = dpre[0].shape[2]
    step = width // groups
    count, rows, _ = out[0].shape
    count //= len(turns)
    across = (((0,), (0,)), ((), ()))
    mine = lax.rem(place[1], cores)
    for i, turn in enumerate(turns):
        other = lax.rem(place[0] + turn, groups) if cores == 1 else place[0] ^ turn
        at = other * step
        cols = pl.ds(pl.multiple_of(at, step), step)
        for ours, others, wide in (
            ([x], dpre, slice(0, width)),
            (acts, dpred, slice(width, None)),
        ):
            total = None
            first = 0
            for other in others:
                here, cells, columns = other.shape
                value = [ref[first : first + here, :, cols] for ref in ours]
                value = (jnp.concatenate(value, axis=1) if len(value) > 1 else value[0])
                first += here
                part = lax.dot_general(
                    value.reshape(here * cells, step),
                    other[...].reshape(here * cells, columns),
                    across,
                    preferred_element_type=F32,
                )
                total = part if total is None else total + part
            total = total.astype(BF16).reshape(count, cores, rows, total.shape[1])
            for b in range(count):
                block = [total[b, c] for c in range(cores)]
                if cores == 1:
                    out[0][i * count + b, :, wide] = block[0]
                else:
                    low = mine == 0
                    out[0][i * count + b, :, wide] = jnp.where(low, block[1], block[0])
                    out[1][i * count + b, :, wide] = jnp.where(low, block[0], block[1])


def weights(x, act, dpre, dpred, place, blocks, groups, cores, turns):
    width = x[0].shape[2]
    columns = width + dpred[0].shape[2]
    rows = width // blocks
    count = len(turns) * blocks // (groups * cores)
    counts = [len(x), len(act), len(dpre), len(dpred)]
    return pl.pallas_call(
        functools.partial(weights_kernel, turns, groups, cores, counts),
        in_specs=[ON_SMEM] + [ON_VMEM] * sum(counts),
        out_specs=[ON_VMEM] * cores,
        out_shape=[pltpu.VMEM((count, rows, columns), BF16)] * cores,
        compiler_params=params(),
        cost_estimate=cost(1000, 1000),
        name="weights",
    )(place, *x, *act, *dpre, *dpred)


def plus(left, right):
    return (left.astype(F32) + right.astype(F32)).astype(BF16)


def add_kernel(kept_ref, came_ref, out):
    for i in range(out.shape[0]):
        out[i] = plus(kept_ref[i], came_ref[i])


def add(kept, came):
    return pl.pallas_call(
        add_kernel,
        in_specs=[ON_VMEM] * 2,
        out_specs=ON_VMEM,
        out_shape=pltpu.VMEM(kept.shape, BF16),
        compiler_params=params(),
        cost_estimate=cost(1000, 1000),
        name="add",
    )(kept, came)


def outer_kernel(kept_ref, came_ref, near_ref, far_ref, near_kept, far_kept):
    chips = kept_ref.shape[0] // 3
    half = chips // 2
    for c in range(chips):
        one, two, three = (
            plus(kept_ref[t * chips + c], came_ref[t * chips + c]) for t in range(3)
        )
        if c < half:
            near_ref[c], near_ref[half + c], near_kept[c] = one, three, two
        else:
            far_ref[c - half], far_ref[c], far_kept[c - half] = two, three, one


def inner_kernel(near_kept, near_came, far_kept, far_came, near_ref, far_ref):
    half = near_ref.shape[0]
    for c in range(half):
        near_ref[c] = plus(near_kept[c], near_came[half + c])
        far_ref[c] = plus(far_kept[c], far_came[half + c])


def paired(kernel, given, counts):
    _, rows, columns = given[0].shape
    return pl.pallas_call(
        kernel,
        in_specs=[ON_VMEM] * len(given),
        out_specs=[ON_VMEM] * len(counts),
        out_shape=[pltpu.VMEM((count, rows, columns), BF16) for count in counts],
        compiler_params=params(),
        cost_estimate=cost(1000, 1000),
        name="pairs",
    )(*given)


def chips_kernel(parts, place, own, near, far, near_last, far_last, *out):
    half = near_last.shape[0]
    mine = lax.rem(place[1] // 2, parts)
    total = []
    for c in range(parts):
        pair = (near, near_last) if c < half else (far, far_last)
        total.append(sum((ref[c % half].astype(F32) for ref in pair), own[c].astype(F32)).astype(BF16))
    for s in range(parts):
        to = lax.rem(mine + s, parts)
        value = total[0]
        for c in range(1, parts):
            value = jnp.where(to == c, total[c], value)
        out[s][0] = value


def by_chip(given, place, parts):
    _, rows, columns = given[0].shape
    return pl.pallas_call(
        functools.partial(chips_kernel, parts),
        in_specs=[ON_SMEM] + [ON_VMEM] * len(given),
        out_specs=[ON_VMEM] * parts,
        out_shape=[pltpu.VMEM((1, rows, columns), BF16)] * parts,
        compiler_params=params(),
        cost_estimate=cost(1000, 1000),
        name="chips",
    )(place, *given)


def total_kernel(*refs):
    given, (hidden_ref, output_ref) = refs[:-2], refs[-2:]
    width = hidden_ref.shape[1]
    for ref, cols in ((hidden_ref, slice(0, width)), (output_ref, slice(width, None))):
        total = given[0][0, :, cols].astype(F32)
        for other in given[1:]:
            total = total + other[0, :, cols].astype(F32)
        ref[...] = total


def last_total(given, width):
    _, rows, columns = given[0].shape
    return pl.pallas_call(
        total_kernel,
        in_specs=[ON_VMEM] * len(given),
        out_specs=[ON_VMEM] * 2,
        out_shape=[
            jax.ShapeDtypeStruct((rows, width), F32),
            jax.ShapeDtypeStruct((rows, columns - width), F32),
        ],
        compiler_params=params(),
        cost_estimate=cost(1000, 1000),
        name="total",
    )(*given)


def weight_gradients(x, act, dpre, dpred, place, after, meanwhile):
    groups, regions = lax.axis_size("member"), lax.axis_size("region")
    blocks, width = groups * regions, x[0].shape[2]
    chips = regions // 2
    if groups != 4 or regions % 4 or width % (blocks * 16):
        turns = list(range(groups))
        (part,) = weights(x, act, dpre, dpred, place * 0, blocks, groups, 1, turns)
        part = part.reshape(width, -1)
        part = lax.psum_scatter(part, "member", scatter_dimension=0, tiled=True)
        part = lax.psum_scatter(part, "region", scatter_dimension=0, tiled=True).astype(F32)
        return part[:, :width], part[:, width:], meanwhile(dpre)
    away, kept = weights(x, act, dpre, dpred, place, blocks, groups, 2, [1, 2, 3])
    (away, kept), _ = lax.optimization_barrier(((away, kept), after))
    came = exchanged(away, "region", 1)
    half = chips // 2
    near, far, near_kept, far_kept = paired(outer_kernel, (kept, came), (chips, chips, half, half))
    away, kept = weights(x, act, dpre, dpred, place, blocks, groups, 2, [0])
    own = add(kept, exchanged(away, "region", 1))
    near, far = exchanged(near, "member", 1), exchanged(far, "member", 2)
    dpre, _ = lax.optimization_barrier((dpre, own))
    done = meanwhile(dpre)
    near_last, far_last = paired(inner_kernel, (near_kept, near, far_kept, far), (half, half))
    near_last = exchanged(near_last, "member", 2)
    far_last = exchanged(far_last, "member", 1)
    given = (own, near, far, near_last, far_last)
    given, done = lax.optimization_barrier((given, done))
    parts = by_chip(given, place, chips)
    given = [parts[0]]
    for s in range(1, chips):
        route = [(i, (i + 2 * s) % regions) for i in range(regions)]
        given.append(lax.ppermute(parts[s], "region", route))
    return *last_total(given, width), done


def finish_kernel(first, own_ref, up_ref, down_ref, w_ref, *refs):
    out_ref, slots, sems = refs[-3:]
    copies = []
    for m in range(own_ref.shape[0]):
        total = own_ref[m].astype(F32) + up_ref[m].astype(F32) + down_ref[m].astype(F32)
        slots[m] = jnp.dot(total.astype(BF16), w_ref[...], preferred_element_type=F32)
        copies.append(pltpu.make_async_copy(slots.at[m], out_ref.at[first + m], sems.at[m]))
        copies[m].start()
    for copy in copies:
        copy.wait()


def finish(first, members, own, up, down, w_hidden_t, held):
    here, nodes, width = own.shape
    extra = [] if held is None else [held]
    return pl.pallas_call(
        functools.partial(finish_kernel, first),
        in_specs=[ON_VMEM] * 4 + [ANYWHERE] * len(extra),
        out_specs=ANYWHERE,
        out_shape=jax.ShapeDtypeStruct((members, nodes, width), F32),
        scratch_shapes=[pltpu.VMEM(own.shape, F32), pltpu.SemaphoreType.DMA((here,))],
        input_output_aliases={4: 0} if extra else {},
        compiler_params=params(),
        cost_estimate=cost(1000, 1000),
        name="finish",
    )(own, up, down, w_hidden_t, *extra)


def body(
    grid_input, w_hidden, b_hidden, w_out, b_out, target, channel_weight, interp_weight, block_index
):
    members, cells, width = grid_input.shape
    groups, regions = lax.axis_size("member"), lax.axis_size("region")
    per_region = MBLK_REG
    place = jnp.stack([lax.axis_index("member"), lax.axis_index("region")]).astype(jnp.int32)
    w_out_t = w_out.T
    x, w_hidden, w_out_t, act, slope, sends = forward(
        grid_input, w_hidden, b_hidden, w_out_t, place, groups
    )
    tiles, own_tiles, w_hidden_t = tiles_matrix(
        interp_weight, block_index, w_hidden, place, per_region, regions
    )
    x = [x]
    given = [sends[0]] + [shifted(sends[s], "member", s) for s in range(1, groups)]
    given, tiles = lax.optimization_barrier((given, tiles))
    parts = shares(members)
    adjoint = score(given, target, b_out, channel_weight, place, parts)
    dpred, dpre, up, down = [], [], [], []
    first = 0
    for i, per in enumerate(parts):
        mine = adjoint[i * groups : (i + 1) * groups]
        back = [mine[0]] + [shifted(mine[s], "member", -s) for s in range(1, groups)]
        if dpred:
            back, _ = lax.optimization_barrier((back, dpred[-1]))
        if dpred:
            back, _ = lax.optimization_barrier((back, dpred[-1]))
        one = backward(first, per, back, w_out_t, slope, tiles, place)
        first += per
        dpred.append(one[0])
        dpre.append(one[1])
        down.append(shifted(one[2], "region", -1))
        up.append(shifted(one[3], "region", 1))

    def meanwhile(dpre):
        own = [own_terms(own_tiles, part) for part in dpre]
        return own, finish(0, members, own[0], up[0], down[0], w_hidden_t, None)

    hidden, output, (own, out) = weight_gradients(
        x, act, dpre, dpred, place, (up[0], down[0]), meanwhile
    )
    first = parts[0]
    for i, per in list(enumerate(parts))[1:]:
        out = finish(first, members, own[i], up[i], down[i], w_hidden_t, out)
        first += per
    return hidden, output, out


def shares(members):
    return [1, 3]


def solution(mesh):
    placed = (
        P("member", "region", None),
        P(),
        P(),
        P(),
        P(),
        P(None, "region"),
        P(),
        P("region", None, None, None),
        P("region", None),
    )
    return jax.shard_map(
        body,
        mesh=mesh,
        in_specs=placed,
        out_specs=(
            P(("member", "region"), None),
            P(("member", "region"), None),
            P("member", "region", None),
        ),
        check_vma=False,
    )
```

```python
import functools

import jax
import jax.numpy as jnp
from jax import lax
from jax.experimental import pallas as pl
from jax.experimental.pallas import tpu as pltpu
from jax.sharding import PartitionSpec as P

ALPHA = 0.95
SMOOTH = 0.25
MBLK_REG = 2
SCOPED = 16 * 1024 * 1024
F32 = jnp.float32
BF16 = jnp.bfloat16
ON_VMEM = pl.BlockSpec(memory_space=pltpu.VMEM)
ON_HBM = pl.BlockSpec(memory_space=pltpu.HBM)
ON_SMEM = pl.BlockSpec(memory_space=pltpu.SMEM)
ANYWHERE = pl.BlockSpec(memory_space=pl.ANY)


def shifted(block, axis, distance):
    count = lax.axis_size(axis)
    return lax.ppermute(block, axis, [((i - distance) % count, i) for i in range(count)])


def exchanged(block, axis, bit):
    count = lax.axis_size(axis)
    return lax.ppermute(block, axis, [(i, i ^ bit) for i in range(count)])


def smooth_slope(diff):
    return diff * lax.rsqrt(diff * diff + SMOOTH * SMOOTH)


def params():
    return pltpu.CompilerParams(vmem_limit_bytes=SCOPED)


def in_hbm(array):
    return pltpu.with_memory_space_constraint(array, pltpu.HBM)


def cost(flops, moved):
    return pl.CostEstimate(flops=int(flops), bytes_accessed=int(moved), transcendentals=0)


def cells_forward(
    turn, place, pieces, x_ref, w_ref, b_ref, wout_ref, act_ref, slope_ref, send_ref, ready
):
    members, cells, width = x_ref.shape
    length = cells // pieces
    at = lax.rem(place[0] + turn, pieces) * length
    cells = pl.ds(pl.multiple_of(at, length), length)
    each = 2 if members % 2 == 0 else 1
    starts = range(0, members, each)
    lines = dict.fromkeys(starts)
    step = width // len(ready)
    for part, wait in enumerate(ready):
        wait()
        cols = slice(part * step, (part + 1) * step)
        for m in starts:
            rows = x_ref[m : m + each, cells, :].reshape(each * length, width)
            pre = jnp.dot(rows, w_ref[:, cols], preferred_element_type=F32) + b_ref[:, cols]
            logistic = 0.5 * jnp.tanh(0.5 * pre) + 0.5
            act = pre * logistic
            slope = (logistic + act * (1.0 - logistic)).astype(BF16)
            slope_ref[m : m + each, :, cols] = slope.reshape(each, length, step)
            act = act.astype(BF16)
            act_ref[m : m + each, :, cols] = act.reshape(each, length, step)
            line = lax.dot_general(
                wout_ref[:, cols], act, (((1,), (1,)), ((), ())), preferred_element_type=F32
            )
            lines[m] = line if lines[m] is None else lines[m] + line
    first = lines[0][:, :length].astype(BF16)
    send_ref[0] = first
    base = first.astype(F32)
    for m in starts:
        for i in range(each):
            line = lines[m][:, i * length : (i + 1) * length]
            send_ref[1 + m + i] = (line - base).astype(BF16)


def first_kernel(
    turn, pieces, place, x_hbm, w_hbm, b_hbm, wout_hbm, x_ref, w_ref, b_ref, wout_ref,
    act_ref, slope_ref, send_ref, x_sems, sems
):
    length = x_ref.shape[1] // pieces
    x_copies = []
    for s in range(pieces):
        at = lax.rem(place[0] + turn + s, pieces) * length
        cells = pl.ds(pl.multiple_of(at, length), length)
        x_copies.append(
            pltpu.make_async_copy(x_hbm.at[:, cells, :], x_ref.at[:, cells, :], x_sems.at[s])
        )
    half = w_ref.shape[1] // 2
    w_copies = []
    for i in range(2):
        cols = slice(i * half, (i + 1) * half)
        w_copies.append(pltpu.make_async_copy(w_hbm.at[:, cols], w_ref.at[:, cols], sems.at[2 + i]))
    small = [
        pltpu.make_async_copy(b_hbm, b_ref, sems.at[0]),
        pltpu.make_async_copy(wout_hbm, wout_ref, sems.at[1]),
    ]
    early = small + w_copies[:1] + x_copies[:1]
    for copy in early + w_copies[1:]:
        copy.start()

    def first_half():
        for copy in early:
            copy.wait()
        for copy in x_copies[1:]:
            copy.start()

    def second_half():
        w_copies[1].wait()

    cells_forward(
        turn, place, pieces, x_ref, w_ref, b_ref, wout_ref, act_ref, slope_ref, send_ref,
        [first_half, second_half],
    )
    for copy in x_copies[1:]:
        copy.wait()


def later_kernel(turn, pieces, place, x_ref, w_ref, b_ref, wout_ref, act_ref, slope_ref, send_ref):
    cells_forward(
        turn, place, pieces, x_ref, w_ref, b_ref, wout_ref, act_ref, slope_ref, send_ref,
        [lambda: None],
    )


def forward(grid_input, w_hidden, b_hidden, w_out_t, place, pieces):
    members, cells, width = grid_input.shape
    channels = w_out_t.shape[0]
    length = cells // pieces
    rows = pltpu.VMEM((members, length, width), BF16)
    results = [rows, rows, pltpu.VMEM((members + 1, channels, length), BF16)]
    turns = far_first(pieces)
    estimate = cost(1000, 1000)
    x, w, b, w_out, *one = pl.pallas_call(
        functools.partial(first_kernel, turns[0], pieces),
        in_specs=[ON_SMEM] + [ON_HBM] * 4,
        out_specs=[ON_VMEM] * 7,
        out_shape=[
            pltpu.VMEM(grid_input.shape, BF16),
            pltpu.VMEM(w_hidden.shape, BF16),
            pltpu.VMEM((1, width), F32),
            pltpu.VMEM(w_out_t.shape, BF16),
        ]
        + results,
        scratch_shapes=[pltpu.SemaphoreType.DMA((pieces,)), pltpu.SemaphoreType.DMA((4,))],
        compiler_params=params(),
        cost_estimate=estimate,
        name="forward",
    )(place, in_hbm(grid_input), in_hbm(w_hidden), in_hbm(b_hidden.reshape(1, width)), in_hbm(w_out_t))
    done = {turns[0]: one}
    for turn in turns[1:]:
        b, _ = lax.optimization_barrier((b, one[2]))
        one = pl.pallas_call(
            functools.partial(later_kernel, turn, pieces),
            in_specs=[ON_SMEM] + [ON_VMEM] * 4,
            out_specs=[ON_VMEM] * 3,
            out_shape=results,
            compiler_params=params(),
            cost_estimate=estimate,
            name="forward",
        )(place, x, w, b, w_out)
        done[turn] = one
    act, slope, sends = zip(*(done[s] for s in range(pieces)))
    return x, w, w_out, list(act), list(slope), list(sends)


def far_first(pieces):
    return sorted(range(pieces), key=lambda s: (s == 0, -min(s, pieces - s), s))


def score_kernel(pieces, place, target_ref, bias_ref, weight_ref, *refs):
    given, out, (bias, weights_of) = refs[:pieces], refs[pieces:-2], refs[-2:]
    extra, channels, length = given[0].shape
    per = extra - 1
    members = per * pieces
    kappa = ALPHA / (2.0 * members * (members - 1)) + (1.0 - ALPHA) / (2.0 * members * members)
    start = pl.multiple_of(place[0] * length, length)
    bias[...] = jnp.broadcast_to(bias_ref[...], (8, channels)).T
    weights_of[...] = jnp.broadcast_to(weight_ref[...], (8, channels)).T

    def rows_step(i, carry):
        rows = pl.ds(pl.multiple_of(i * 16, 16), 16)
        own = []
        for s in range(pieces):
            base = given[s][0, rows, :].astype(F32)
            own += [base + given[s][m, rows, :].astype(F32) for m in range(1, extra)]
        aim = target_ref[rows, pl.ds(start, length)] - bias[rows, :1]
        weight = weights_of[rows, :1]
        halves = []
        for half in (slice(0, 8), slice(8, 16)):
            mine = [value[half] for value in own]
            spread = [None] * members
            for j in range(members):
                for k in range(j + 1, members):
                    slope = smooth_slope(mine[j] - mine[k])
                    spread[j] = slope if spread[j] is None else spread[j] + slope
                    spread[k] = -slope if spread[k] is None else spread[k] - slope
            skill = [smooth_slope(value - aim[half]) * (1.0 / members) for value in mine]
            halves.append(
                [weight[half] * (a - (2.0 * kappa) * b) for a, b in zip(skill, spread)]
            )
        for j in range(members):
            part = j % per
            at = j // per
            while part >= out[at].shape[0]:
                part -= out[at].shape[0]
                at += pieces
            value = jnp.concatenate([half[j] for half in halves], axis=0)
            out[at][part, rows, :] = value.astype(BF16)
        return carry

    lax.fori_loop(0, channels // 16, rows_step, 0)


def score(given, target, b_out, channel_weight, place, parts):
    pieces = len(given)
    extra, channels, length = given[0].shape
    shapes = [pltpu.VMEM((part, channels, length), BF16) for part in parts for _ in given]
    return pl.pallas_call(
        functools.partial(score_kernel, pieces),
        in_specs=[ON_SMEM] + [ON_VMEM] * (3 + pieces),
        out_specs=[ON_VMEM] * len(shapes),
        out_shape=shapes,
        scratch_shapes=[pltpu.VMEM((channels, 8), F32)] * 2,
        compiler_params=params(),
        cost_estimate=cost(40_000_000, 1 << 20),
        name="score",
    )(place, target, b_out.reshape(1, channels), channel_weight.reshape(1, channels), *given)


def tiles_kernel(per_region, regions, place, index_ref, tile_ref, w_ref, out_ref, own_ref, w_t_ref, total):
    blocks, sources, cells, nodes = tile_ref.shape
    total[...] = jnp.zeros_like(total)
    for b in range(blocks):
        for k in range(sources):
            number = index_ref[b, k]
            relative = lax.rem(number // per_region - place[1] + 1 + regions, regions)
            slot = relative * per_region + lax.rem(number, per_region)
            total[slot, b] += tile_ref[b, k].astype(F32).T
    for s in range(total.shape[0]):
        ref, to = (own_ref, s - per_region) if s // per_region == 1 else (out_ref, s if s < per_region else s - per_region)
        for b in range(blocks):
            ref[to * nodes : (to + 1) * nodes, b * cells : (b + 1) * cells] = total[s, b].astype(BF16)
    step = 256
    for lo in range(0, w_ref.shape[0], step):
        w_t_ref[:, lo : lo + step] = w_ref[lo : lo + step, :].T


def tiles_matrix(interp_weight, block_index, w_hidden, place, per_region, regions):
    blocks, _, cells, nodes = interp_weight.shape
    slots = 3 * per_region
    return pl.pallas_call(
        functools.partial(tiles_kernel, per_region, regions),
        in_specs=[ON_SMEM, ON_SMEM, ON_VMEM, ON_VMEM],
        out_specs=[ON_VMEM] * 3,
        out_shape=[
            pltpu.VMEM((2 * per_region * nodes, blocks * cells), BF16),
            pltpu.VMEM((per_region * nodes, blocks * cells), BF16),
            pltpu.VMEM(w_hidden.shape, BF16),
        ],
        scratch_shapes=[pltpu.VMEM((slots, blocks, nodes, cells), F32)],
        compiler_params=params(),
        cost_estimate=cost(4_000_000, 2 << 20),
        name="tiles",
    )(place, block_index, interp_weight, w_hidden)


def backward_kernel(first, pieces, place, wout_ref, tiles_ref, *refs):
    given, slopes = refs[:pieces], refs[pieces : 2 * pieces]
    dpred_ref, dpre_ref, below_ref, above_ref = refs[2 * pieces :]
    length = given[0].shape[2]
    members, nodes, width = below_ref.shape
    step = 512
    for m in range(members):
        for s in range(pieces):
            rows = slice(s * length, (s + 1) * length)
            dpred_ref[m, rows, :] = given[s][m].astype(F32).T.astype(BF16)
        for lo in range(0, width, step):
            cols = slice(lo, lo + step)
            dact = jnp.dot(dpred_ref[m], wout_ref[:, cols], preferred_element_type=F32)
            for s in range(pieces):
                slope = slopes[s][first + m, :, cols].astype(F32)
                dpre = (dact[s * length : (s + 1) * length] * slope).astype(BF16)
                at = lax.rem(place[0] + s, pieces) * length
                dpre_ref[m, pl.ds(pl.multiple_of(at, length), length), cols] = dpre
            terms = jnp.dot(tiles_ref[...], dpre_ref[m, :, cols], preferred_element_type=F32)
            below_ref[m, :, cols] = terms[:nodes].astype(BF16)
            above_ref[m, :, cols] = terms[nodes:].astype(BF16)


def backward(first, members, given, w_out_t, slope, tiles, place):
    pieces = len(given)
    _, length, width = slope[0].shape
    cells = length * pieces
    channels = w_out_t.shape[0]
    nodes = tiles.shape[0] // 2
    return pl.pallas_call(
        functools.partial(backward_kernel, first, pieces),
        in_specs=[ON_SMEM] + [ON_VMEM] * (2 + pieces + len(slope)),
        out_specs=[ON_VMEM] * 4,
        out_shape=[
            pltpu.VMEM((members, cells, channels), BF16),
            pltpu.VMEM((members, cells, width), BF16),
            pltpu.VMEM((members, nodes, width), BF16),
            pltpu.VMEM((members, nodes, width), BF16),
        ],
        compiler_params=params(),
        cost_estimate=cost(2 * members * cells * width * (256 + 3 * nodes), 5 << 20),
        name="backward",
    )(place, w_out_t, tiles, *given, *slope)


def own_kernel(tiles_ref, dpre_ref, out_ref):
    for m in range(dpre_ref.shape[0]):
        out_ref[m] = jnp.dot(tiles_ref[...], dpre_ref[m], preferred_element_type=F32)


def own_terms(tiles, dpre):
    members, cells, width = dpre.shape
    return pl.pallas_call(
        own_kernel,
        in_specs=[ON_VMEM] * 2,
        out_specs=ON_VMEM,
        out_shape=pltpu.VMEM((members, tiles.shape[0], width), F32),
        compiler_params=params(),
        cost_estimate=cost(1000, 1000),
        name="own",
    )(tiles, dpre)


def weights_kernel(turns, groups, cores, counts, place, *refs):
    split_at, lists = 0, []
    for count in counts:
        lists.append(refs[split_at : split_at + count])
        split_at += count
    (x,), acts, dpre, dpred = lists
    out = refs[split_at:]
    width = dpre[0].shape[2]
    step = width // groups
    count, rows, _ = out[0].shape
    count //= len(turns)
    across = (((0,), (0,)), ((), ()))
    mine = lax.rem(place[1], cores)
    for i, turn in enumerate(turns):
        other = lax.rem(place[0] + turn, groups) if cores == 1 else place[0] ^ turn
        at = other * step
        cols = pl.ds(pl.multiple_of(at, step), step)
        for ours, others, wide in (
            ([x], dpre, slice(0, width)),
            (acts, dpred, slice(width, None)),
        ):
            total = None
            first = 0
            for other in others:
                here, cells, columns = other.shape
                value = [ref[first : first + here, :, cols] for ref in ours]
                value = (jnp.concatenate(value, axis=1) if len(value) > 1 else value[0])
                first += here
                part = lax.dot_general(
                    value.reshape(here * cells, step),
                    other[...].reshape(here * cells, columns),
                    across,
                    preferred_element_type=F32,
                )
                total = part if total is None else total + part
            total = total.astype(BF16).reshape(count, cores, rows, total.shape[1])
            for b in range(count):
                block = [total[b, c] for c in range(cores)]
                if cores == 1:
                    out[0][i * count + b, :, wide] = block[0]
                else:
                    low = mine == 0
                    out[0][i * count + b, :, wide] = jnp.where(low, block[1], block[0])
                    out[1][i * count + b, :, wide] = jnp.where(low, block[0], block[1])


def weights(x, act, dpre, dpred, place, blocks, groups, cores, turns):
    width = x[0].shape[2]
    columns = width + dpred[0].shape[2]
    rows = width // blocks
    count = len(turns) * blocks // (groups * cores)
    counts = [len(x), len(act), len(dpre), len(dpred)]
    return pl.pallas_call(
        functools.partial(weights_kernel, turns, groups, cores, counts),
        in_specs=[ON_SMEM] + [ON_VMEM] * sum(counts),
        out_specs=[ON_VMEM] * cores,
        out_shape=[pltpu.VMEM((count, rows, columns), BF16)] * cores,
        compiler_params=params(),
        cost_estimate=cost(1000, 1000),
        name="weights",
    )(place, *x, *act, *dpre, *dpred)


def plus(left, right):
    return (left.astype(F32) + right.astype(F32)).astype(BF16)


def add_kernel(kept_ref, came_ref, out):
    for i in range(out.shape[0]):
        out[i] = plus(kept_ref[i], came_ref[i])


def add(kept, came):
    return pl.pallas_call(
        add_kernel,
        in_specs=[ON_VMEM] * 2,
        out_specs=ON_VMEM,
        out_shape=pltpu.VMEM(kept.shape, BF16),
        compiler_params=params(),
        cost_estimate=cost(1000, 1000),
        name="add",
    )(kept, came)


def outer_kernel(kept_ref, came_ref, near_ref, far_ref, near_kept, far_kept):
    chips = kept_ref.shape[0] // 3
    half = chips // 2
    for c in range(chips):
        one, two, three = (
            plus(kept_ref[t * chips + c], came_ref[t * chips + c]) for t in range(3)
        )
        if c < half:
            near_ref[c], near_ref[half + c], near_kept[c] = one, three, two
        else:
            far_ref[c - half], far_ref[c], far_kept[c - half] = two, three, one


def inner_kernel(near_kept, near_came, far_kept, far_came, near_ref, far_ref):
    half = near_ref.shape[0]
    for c in range(half):
        near_ref[c] = plus(near_kept[c], near_came[half + c])
        far_ref[c] = plus(far_kept[c], far_came[half + c])


def paired(kernel, given, counts):
    _, rows, columns = given[0].shape
    return pl.pallas_call(
        kernel,
        in_specs=[ON_VMEM] * len(given),
        out_specs=[ON_VMEM] * len(counts),
        out_shape=[pltpu.VMEM((count, rows, columns), BF16) for count in counts],
        compiler_params=params(),
        cost_estimate=cost(1000, 1000),
        name="pairs",
    )(*given)


def chips_kernel(parts, place, own, near, far, near_last, far_last, *out):
    half = near_last.shape[0]
    mine = lax.rem(place[1] // 2, parts)
    total = []
    for c in range(parts):
        pair = (near, near_last) if c < half else (far, far_last)
        total.append(sum((ref[c % half].astype(F32) for ref in pair), own[c].astype(F32)).astype(BF16))
    for s in range(parts):
        to = lax.rem(mine + s, parts)
        value = total[0]
        for c in range(1, parts):
            value = jnp.where(to == c, total[c], value)
        out[s][0] = value


def by_chip(given, place, parts):
    _, rows, columns = given[0].shape
    return pl.pallas_call(
        functools.partial(chips_kernel, parts),
        in_specs=[ON_SMEM] + [ON_VMEM] * len(given),
        out_specs=[ON_VMEM] * parts,
        out_shape=[pltpu.VMEM((1, rows, columns), BF16)] * parts,
        compiler_params=params(),
        cost_estimate=cost(1000, 1000),
        name="chips",
    )(place, *given)


def total_kernel(*refs):
    given, (hidden_ref, output_ref) = refs[:-2], refs[-2:]
    width = hidden_ref.shape[1]
    for ref, cols in ((hidden_ref, slice(0, width)), (output_ref, slice(width, None))):
        total = given[0][0, :, cols].astype(F32)
        for other in given[1:]:
            total = total + other[0, :, cols].astype(F32)
        ref[...] = total


def last_total(given, width):
    _, rows, columns = given[0].shape
    return pl.pallas_call(
        total_kernel,
        in_specs=[ON_VMEM] * len(given),
        out_specs=[ON_VMEM] * 2,
        out_shape=[
            jax.ShapeDtypeStruct((rows, width), F32),
            jax.ShapeDtypeStruct((rows, columns - width), F32),
        ],
        compiler_params=params(),
        cost_estimate=cost(1000, 1000),
        name="total",
    )(*given)


def weight_gradients(x, act, dpre, dpred, place, after, meanwhile):
    groups, regions = lax.axis_size("member"), lax.axis_size("region")
    blocks, width = groups * regions, x[0].shape[2]
    chips = regions // 2
    if groups != 4 or regions % 4 or width % (blocks * 16):
        turns = list(range(groups))
        (part,) = weights(x, act, dpre, dpred, place * 0, blocks, groups, 1, turns)
        part = part.reshape(width, -1)
        part = lax.psum_scatter(part, "member", scatter_dimension=0, tiled=True)
        part = lax.psum_scatter(part, "region", scatter_dimension=0, tiled=True).astype(F32)
        return part[:, :width], part[:, width:], meanwhile(dpre)
    away, kept = weights(x, act, dpre, dpred, place, blocks, groups, 2, [1, 2, 3])
    (away, kept), _ = lax.optimization_barrier(((away, kept), after))
    came = exchanged(away, "region", 1)
    half = chips // 2
    near, far, near_kept, far_kept = paired(outer_kernel, (kept, came), (chips, chips, half, half))
    away, kept = weights(x, act, dpre, dpred, place, blocks, groups, 2, [0])
    own = add(kept, exchanged(away, "region", 1))
    near, far = exchanged(near, "member", 1), exchanged(far, "member", 2)
    dpre, _ = lax.optimization_barrier((dpre, own))
    done = meanwhile(dpre)
    near_last, far_last = paired(inner_kernel, (near_kept, near, far_kept, far), (half, half))
    near_last = exchanged(near_last, "member", 2)
    far_last = exchanged(far_last, "member", 1)
    given = (own, near, far, near_last, far_last)
    given, done = lax.optimization_barrier((given, done))
    parts = by_chip(given, place, chips)
    given = [parts[0]]
    for s in range(1, chips):
        route = [(i, (i + 2 * s) % regions) for i in range(regions)]
        given.append(lax.ppermute(parts[s], "region", route))
    return *last_total(given, width), done


def finish_kernel(first, own_ref, up_ref, down_ref, w_ref, *refs):
    out_ref, slots, sems = refs[-3:]
    copies = []
    for m in range(own_ref.shape[0]):
        total = own_ref[m].astype(F32) + up_ref[m].astype(F32) + down_ref[m].astype(F32)
        slots[m] = jnp.dot(total.astype(BF16), w_ref[...], preferred_element_type=F32)
        copies.append(pltpu.make_async_copy(slots.at[m], out_ref.at[first + m], sems.at[m]))
        copies[m].start()
    for copy in copies:
        copy.wait()


def finish(first, members, own, up, down, w_hidden_t, held):
    here, nodes, width = own.shape
    extra = [] if held is None else [held]
    return pl.pallas_call(
        functools.partial(finish_kernel, first),
        in_specs=[ON_VMEM] * 4 + [ANYWHERE] * len(extra),
        out_specs=ANYWHERE,
        out_shape=jax.ShapeDtypeStruct((members, nodes, width), F32),
        scratch_shapes=[pltpu.VMEM(own.shape, F32), pltpu.SemaphoreType.DMA((here,))],
        input_output_aliases={4: 0} if extra else {},
        compiler_params=params(),
        cost_estimate=cost(1000, 1000),
        name="finish",
    )(own, up, down, w_hidden_t, *extra)


def body(
    grid_input, w_hidden, b_hidden, w_out, b_out, target, channel_weight, interp_weight, block_index
):
    members, cells, width = grid_input.shape
    groups, regions = lax.axis_size("member"), lax.axis_size("region")
    per_region = MBLK_REG
    place = jnp.stack([lax.axis_index("member"), lax.axis_index("region")]).astype(jnp.int32)
    w_out_t = w_out.T
    x, w_hidden, w_out_t, act, slope, sends = forward(
        grid_input, w_hidden, b_hidden, w_out_t, place, groups
    )
    tiles, own_tiles, w_hidden_t = tiles_matrix(
        interp_weight, block_index, w_hidden, place, per_region, regions
    )
    x = [x]
    given = [sends[0]] + [shifted(sends[s], "member", s) for s in range(1, groups)]
    given, tiles = lax.optimization_barrier((given, tiles))
    parts = shares(members)
    adjoint = score(given, target, b_out, channel_weight, place, parts)
    dpred, dpre, up, down = [], [], [], []
    first = 0
    for i, per in enumerate(parts):
        mine = adjoint[i * groups : (i + 1) * groups]
        back = [mine[0]] + [shifted(mine[s], "member", -s) for s in range(1, groups)]
        if dpred:
            back, _ = lax.optimization_barrier((back, dpred[-1]))
        if dpred:
            back, _ = lax.optimization_barrier((back, dpred[-1]))
        one = backward(first, per, back, w_out_t, slope, tiles, place)
        first += per
        dpred.append(one[0])
        dpre.append(one[1])
        down.append(shifted(one[2], "region", -1))
        up.append(shifted(one[3], "region", 1))

    def meanwhile(dpre):
        own = [own_terms(own_tiles, part) for part in dpre]
        return own, finish(0, members, own[0], up[0], down[0], w_hidden_t, None)

    hidden, output, (own, out) = weight_gradients(
        x, act, dpre, dpred, place, (up[0], down[0]), meanwhile
    )
    first = parts[0]
    for i, per in list(enumerate(parts))[1:]:
        out = finish(first, members, own[i], up[i], down[i], w_hidden_t, out)
        first += per
    return hidden, output, out


def shares(members):
    return [1, 3]


def solution(mesh):
    placed = (
        P("member", "region", None),
        P(),
        P(),
        P(),
        P(),
        P(None, "region"),
        P(),
        P("region", None, None, None),
        P("region", None),
    )
    return jax.shard_map(
        body,
        mesh=mesh,
        in_specs=placed,
        out_specs=(
            P(("member", "region"), None),
            P(("member", "region"), None),
            P("member", "region", None),
        ),
        check_vma=False,
    )
```
